256 devices in a mesh: dp: 8 (over z_lo, y), ctx: 32 (over x, z_hi, core).
Axes of the slice: x: 4, y: 4, z: 8 (z_hi: 4, z_lo: 2; z = z_hi * 2 + z_lo), core: 2. Of those that a mesh axis runs over, the one named last changes fastest.
Arguments:
- query_in: bfloat16 [8, 4096, 1024], P('dp', 'ctx'), may hold values from -170 to 170
- key_in: bfloat16 [8, 4096, 1024], P('dp', 'ctx'), may hold values from -4.6 to 4.6
- value_in: bfloat16 [8, 4096, 1024], P('dp', 'ctx'), may hold values from -6 to 6
- residual: bfloat16 [8, 4096, 1920], P('dp', 'ctx'), may hold values from -6 to 6
- w_out: bfloat16 [1024, 1920], replicated, may hold values from -0.1875 to 0.1875
- norm_gain: float32 [1920], replicated, may hold values from 0.25 to 1.75
- short_taps: float32 [3, 7, 1920], replicated, may hold values from -4 to 4
- filters: bfloat16 [15, 128], replicated, may hold values from -1.25 to 1.25
- skip_gain: float32 [1920], replicated, may hold values from -1 to 1
- cotangent: bfloat16 [8, 4096, 1920], P('dp', 'ctx'), may hold values from -6 to 6
Outputs:
- layer_out: bfloat16 [8, 4096, 1920], P('dp', 'ctx')
- grad_residual: bfloat16 [8, 4096, 1920], P('dp', 'ctx')
- grad_query: bfloat16 [8, 4096, 1024], P('dp', 'ctx')
- grad_key: bfloat16 [8, 4096, 1024], P('dp', 'ctx')
- grad_value: bfloat16 [8, 4096, 1024], P('dp', 'ctx')
- grad_weight: float32 [1024, 1920], P('dp', 'ctx')
- grad_gain: float32 [1920], replicated
- grad_taps: float32 [3, 7, 1920], replicated
- grad_filters: float32 [15, 128], replicated
- grad_skip: float32 [1920], replicated
The draws below stay inside these ranges and needn't reach their ends.
All inputs are finite; a program needn't handle non-finite values.
Results may differ from the reference program's by a relative error of at most 0.029.
Values may be sent and summed in bfloat16 or wider, within the bound.
No kernel may reach another device: no remote copies, remote signals or barrier semaphores. Data moves between devices by JAX's collectives and lax.ppermute only.
A program may use at most 128 MiB of HBM per device.

```python
import jax
import jax.numpy as jnp
from jax import lax

D = 1920
HEADS = 8
HDIM = 128
SHORT = 7
LONG = 128
FCH = 128
SEQ = 4096
BATCH = 8
AD = 1024
FILTERS = 15


def paired_rows(key):
    full_shape = (BATCH, SEQ, HEADS * HDIM)
    base_query = jnp.clip(jax.random.normal(jax.random.fold_in(key, 101), full_shape, jnp.float32), -4.5, 4.5)
    base_key = jnp.clip(jax.random.normal(jax.random.fold_in(key, 202), full_shape, jnp.float32), -4.5, 4.5)
    return (base_query.astype(jnp.bfloat16), base_key.astype(jnp.bfloat16))


def draw_query_in(key, part):
    both_rows = paired_rows(key)
    return both_rows[0]


def draw_key_in(key, part):
    both_rows = paired_rows(key)
    return both_rows[1]


def block_levels(key, shape, pieces, low, high):
    def one(axis_at, parts):
        draws = jax.random.uniform(jax.random.fold_in(jax.random.fold_in(key, 6), axis_at), (parts,), jnp.float32, low / len(pieces), high / len(pieces))
        return jnp.repeat(jnp.exp(draws), shape[axis_at] // parts).reshape((-1,) + (1,) * (len(shape) - axis_at - 1))

    loudness = one(*pieces[0])
    for cut in pieces[1:]:
        loudness = loudness * one(*cut)
    return loudness


def gaussian(stream_key, dims, spread, limit, shards=(), kind=jnp.bfloat16):
    values = spread * jax.random.normal(stream_key, dims, jnp.float32)
    if shards:
        values = values * block_levels(stream_key, dims, shards, -0.22, 0.18)
    return jnp.clip(values, -limit, limit).astype(kind)


def setup_inputs(seed: int = 0) -> dict:
    seeds = jax.random.split(jax.random.key(seed), 11)
    query_in = draw_query_in(jax.random.fold_in(seeds[10], 71), 0)
    key_in = draw_key_in(jax.random.fold_in(seeds[10], 71), 0)
    value_in = gaussian(seeds[2], (BATCH, SEQ, AD), 1.0, 6.0, ((0, 8), (1, 32)))
    residual = gaussian(seeds[3], (BATCH, SEQ, D), 1.0, 6.0, ((0, 8), (1, 32)))
    w_out = gaussian(seeds[4], (AD, D), AD ** -0.5, 0.1875)
    norm_gain = jnp.clip(1.0 + 0.15 * jax.random.normal(seeds[5], (D,), jnp.float32), 0.25, 1.75)
    short_taps = gaussian(seeds[6], (3, SHORT, D), 0.4, 4.0, (), jnp.float32)
    filters = gaussian(seeds[7], (FILTERS, LONG), 0.09, 1.25)
    skip_gain = jnp.clip(jax.random.uniform(seeds[8], (D,), jnp.float32, -1.0, 1.0), -1.0, 1.0)
    cotangent = gaussian(seeds[9], (BATCH, SEQ, D), 1.0, 6.0, ((0, 8), (1, 32)))
    return dict(query_in=query_in, key_in=key_in, value_in=value_in, residual=residual, w_out=w_out, norm_gain=norm_gain, short_taps=short_taps, filters=filters, skip_gain=skip_gain, cotangent=cotangent)


def long_matrix(filters):
    tap_count = filters.shape[1]
    groups = filters.shape[0]
    zero_fill = jnp.zeros((groups, tap_count), filters.dtype)
    reversed_taps = jnp.concatenate([zero_fill, filters[:, ::-1], zero_fill], axis=1)
    tiled = jnp.tile(reversed_taps, (1, tap_count))
    tiled = tiled[:, :tap_count * (3 * tap_count - 1)].reshape(groups, tap_count, 3 * tap_count - 1)
    return tiled[:, :, tap_count - 1:3 * tap_count - 1]

def diagonal_sums(corr_table):
    groups = corr_table.shape[0]
    tap_count = corr_table.shape[1]
    padded = jnp.pad(corr_table, ((0, 0), (0, 0), (0, tap_count)))
    flat_view = padded.reshape(groups, 3 * tap_count * tap_count)
    flat_view = jnp.pad(flat_view, ((0, 0), (0, tap_count)))
    skewed = flat_view.reshape(groups, tap_count, 3 * tap_count + 1)
    diag_sums = lax.optimization_barrier(jnp.sum(skewed, axis=1))
    return diag_sums[:, 1:tap_count + 1][:, ::-1]

def attend_forward(operands):
    query_rows, key_rows, value_rows = operands
    score_scale = HDIM ** (-0.5)
    block_len = min(512, SEQ)
    out_blocks = []
    lse_blocks = []
    for first_row in range(0, SEQ, block_len):
        key_end = first_row + block_len
        logits = jnp.dot(query_rows[first_row:key_end], key_rows[:key_end].T, preferred_element_type=jnp.float32) * score_scale
        allowed = jnp.arange(first_row, key_end)[:, None] >= jnp.arange(key_end)[None, :]
        logits = jnp.where(allowed, logits, -jnp.inf)
        row_max = lax.optimization_barrier(jnp.max(logits, axis=-1, keepdims=True))
        log_total = row_max + jnp.log(lax.optimization_barrier(jnp.sum(jnp.exp(logits - row_max), axis=-1, keepdims=True)))
        probs_low = jnp.exp(logits - log_total).astype(jnp.bfloat16)
        out_blocks.append(jnp.dot(probs_low, value_rows[:key_end], preferred_element_type=jnp.float32).astype(jnp.bfloat16))
        lse_blocks.append(log_total)
    return (jnp.concatenate(out_blocks, axis=0), jnp.concatenate(lse_blocks, axis=0))

def attend_backward(operands):
    query_rows, key_rows, value_rows, out_rows, log_totals, grad_rows = operands
    score_scale = HDIM ** (-0.5)
    block_len = min(512, SEQ)
    grad_keys = jnp.zeros((SEQ, HDIM), jnp.float32)
    grad_values = jnp.zeros((SEQ, HDIM), jnp.float32)
    dq_blocks = []
    for first_row in range(0, SEQ, block_len):
        key_end = first_row + block_len
        query_block = query_rows[first_row:key_end]
        grad_block = grad_rows[first_row:key_end]
        logits = jnp.dot(query_block, key_rows[:key_end].T, preferred_element_type=jnp.float32) * score_scale
        allowed = jnp.arange(first_row, key_end)[:, None] >= jnp.arange(key_end)[None, :]
        logits = jnp.where(allowed, logits, -jnp.inf)
        probs = jnp.exp(logits - log_totals[first_row:key_end])
        probs_low = probs.astype(jnp.bfloat16)
        grad_probs = jnp.dot(grad_block, value_rows[:key_end].T, preferred_element_type=jnp.float32)
        row_delta = lax.optimization_barrier(jnp.sum(grad_block.astype(jnp.float32) * out_rows[first_row:key_end].astype(jnp.float32), axis=-1, keepdims=True))
        grad_logits = (probs * (grad_probs - row_delta)).astype(jnp.bfloat16)
        dq_blocks.append(jnp.dot(grad_logits, key_rows[:key_end], preferred_element_type=jnp.float32) * score_scale)
        grad_keys = grad_keys.at[:key_end].add(jnp.dot(grad_logits.T, query_block, preferred_element_type=jnp.float32) * score_scale)
        grad_values = grad_values.at[:key_end].add(jnp.dot(probs_low.T, grad_block, preferred_element_type=jnp.float32))
    return (jnp.concatenate(dq_blocks, axis=0), grad_keys, grad_values)

def hyena_sequence(x_one, grad_one, norm_gain, short_taps, filters, skip_gain):
    x_float = x_one.astype(jnp.float32)
    inv_rms = lax.rsqrt(lax.optimization_barrier(jnp.mean(x_float * x_float, axis=-1, keepdims=True)) + 1e-05)
    normed = lax.optimization_barrier((x_float * inv_rms * norm_gain).astype(jnp.bfloat16))
    normed_ext = jnp.concatenate([jnp.zeros((SHORT - 1, D), jnp.bfloat16), normed], axis=0).astype(jnp.float32)
    streams = jnp.zeros((3, SEQ, D), jnp.float32)
    for tap_index in range(SHORT):
        streams = streams + short_taps[:, tap_index, None, :] * normed_ext[None, SHORT - 1 - tap_index:SHORT - 1 - tap_index + SEQ]
    product = lax.optimization_barrier((streams[1] * streams[2]).astype(jnp.bfloat16))
    blocks = SEQ // LONG + 1
    prod_ext = jnp.concatenate([jnp.zeros((LONG, D), jnp.bfloat16), product], axis=0)
    prod_blocks = prod_ext.reshape(blocks, LONG, FILTERS, FCH).astype(jnp.float32)
    matrix = long_matrix(filters).astype(jnp.float32)
    prev_part = matrix[:, :, :LONG]
    cur_part = matrix[:, :, LONG:]
    conv_out = jnp.einsum('gij,bjgc->bigc', prev_part, prod_blocks[:-1]) + jnp.einsum('gij,bjgc->bigc', cur_part, prod_blocks[1:])
    mixed_out = conv_out.reshape(SEQ, D) + skip_gain * product.astype(jnp.float32)
    layer_one = (x_float + streams[0] * mixed_out).astype(jnp.bfloat16)
    grad_out = grad_one.astype(jnp.float32)
    grad_first = grad_out * mixed_out
    grad_mixed = lax.optimization_barrier((grad_out * streams[0]).astype(jnp.bfloat16))
    mix_ext = jnp.concatenate([grad_mixed, jnp.zeros((LONG, D), jnp.bfloat16)], axis=0)
    mix_blocks = mix_ext.reshape(blocks, LONG, FILTERS, FCH).astype(jnp.float32)
    grad_conv = jnp.einsum('gji,bjgc->bigc', cur_part, mix_blocks[:-1]) + jnp.einsum('gji,bjgc->bigc', prev_part, mix_blocks[1:])
    grad_product = grad_conv.reshape(SEQ, D) + skip_gain * grad_mixed.astype(jnp.float32)
    grad_skip = lax.optimization_barrier(jnp.sum(grad_mixed.astype(jnp.float32) * product.astype(jnp.float32), axis=0))
    window = jnp.concatenate([prod_blocks[:-1], prod_blocks[1:]], axis=1)
    corr_table = jnp.einsum('bigc,bjgc->gij', mix_blocks[:-1], window)
    grad_filters = diagonal_sums(corr_table)
    grad_streams = jnp.stack([grad_first, grad_product * streams[2], grad_product * streams[1]])
    stream_ext = jnp.concatenate([grad_streams, jnp.zeros((3, SHORT - 1, D), jnp.float32)], axis=1)
    grad_normed = jnp.zeros((SEQ, D), jnp.float32)
    tap_grads = []
    for tap_index in range(SHORT):
        grad_normed = grad_normed + lax.optimization_barrier(jnp.sum(short_taps[:, tap_index, None, :] * stream_ext[:, tap_index:tap_index + SEQ], axis=0))
        tap_grads.append(lax.optimization_barrier(jnp.sum(grad_streams * normed_ext[None, SHORT - 1 - tap_index:SHORT - 1 - tap_index + SEQ], axis=1)))
    grad_taps = jnp.stack(tap_grads).transpose(1, 0, 2)
    scaled = grad_normed * norm_gain
    grad_gain = lax.optimization_barrier(jnp.sum(grad_normed * x_float * inv_rms, axis=0))
    grad_x = grad_out + inv_rms * (scaled - x_float * inv_rms * inv_rms * lax.optimization_barrier(jnp.mean(scaled * x_float, axis=-1, keepdims=True)))
    return (layer_one, grad_x.astype(jnp.bfloat16), grad_gain, grad_taps, grad_filters, grad_skip)

def split_heads(array):
    return array.reshape(BATCH, SEQ, HEADS, HDIM).transpose(0, 2, 1, 3).reshape(BATCH * HEADS, SEQ, HDIM)

def join_heads(array):
    return array.reshape(BATCH, HEADS, SEQ, HDIM).transpose(0, 2, 1, 3).reshape(BATCH, SEQ, AD)

def reference(query_in, key_in, value_in, residual, w_out, norm_gain, short_taps, filters, skip_gain, cotangent):
    head_query = split_heads(query_in)
    head_key = split_heads(key_in)
    head_value = split_heads(value_in)
    head_out, head_lse = lax.map(attend_forward, (head_query, head_key, head_value))
    attention = join_heads(head_out)
    projected = jnp.einsum('bta,ad->btd', attention.astype(jnp.float32), w_out.astype(jnp.float32))
    x_first = lax.optimization_barrier((residual.astype(jnp.float32) + projected).astype(jnp.bfloat16))

    def one_sequence(inputs):
        return hyena_sequence(inputs[0], inputs[1], norm_gain, short_taps, filters, skip_gain)
    layer_out, grad_residual, gain_parts, tap_parts, filter_parts, skip_parts = lax.map(one_sequence, (x_first, cotangent))
    grad_weight = jnp.einsum('bta,btd->ad', attention.astype(jnp.float32), grad_residual.astype(jnp.float32))
    grad_attention = jnp.einsum('btd,ad->bta', grad_residual.astype(jnp.float32), w_out.astype(jnp.float32)).astype(jnp.bfloat16)
    dq_heads, dk_heads, dv_heads = lax.map(attend_backward, (head_query, head_key, head_value, head_out, head_lse, split_heads(grad_attention)))
    grad_query = join_heads(dq_heads).astype(jnp.bfloat16)
    grad_key = join_heads(dk_heads).astype(jnp.bfloat16)
    grad_value = join_heads(dv_heads).astype(jnp.bfloat16)
    return (layer_out, grad_residual, grad_query, grad_key, grad_value, grad_weight, lax.optimization_barrier(jnp.sum(gain_parts, axis=0)), lax.optimization_barrier(jnp.sum(tap_parts, axis=0)), lax.optimization_barrier(jnp.sum(filter_parts, axis=0)), lax.optimization_barrier(jnp.sum(skip_parts, axis=0)))
```

```python
import jax
import jax.numpy as jnp
from jax import lax
from jax.sharding import Mesh, PartitionSpec as P

D = 1920
HEADS = 8
HDIM = 128
SHORT = 7
LONG = 128
FCH = 128
FILTERS = 15
AD = HEADS * HDIM

DP_AXES = ("zl", "y")
CTX_AXES = ("xa", "xb", "zh", "c")
HEAD_AXES = ("xa", "zh")
SLOT_AXES = ("zl", "y", "xb", "c")


def from_behind(x, by):
    peers = lax.axis_size(CTX_AXES)
    pairs = [(i, i + by) for i in range(peers) if 0 <= i + by < peers]
    return lax.ppermute(x, CTX_AXES, pairs)


def swap(x, axis):
    return lax.ppermute(x, axis, [(0, 1), (1, 0)])


def exchange(x, axes):
    return lax.all_to_all(x, axes, split_axis=0, concat_axis=0, tiled=True)


def long_matrix(filters):
    tap_count = filters.shape[1]
    groups = filters.shape[0]
    zero_fill = jnp.zeros((groups, tap_count), filters.dtype)
    reversed_taps = jnp.concatenate([zero_fill, filters[:, ::-1], zero_fill], axis=1)
    tiled = jnp.tile(reversed_taps, (1, tap_count))
    tiled = tiled[:, : tap_count * (3 * tap_count - 1)].reshape(
        groups, tap_count, 3 * tap_count - 1
    )
    return tiled[:, :, tap_count - 1 : 3 * tap_count - 1]


def diagonal_sums(corr_table):
    groups = corr_table.shape[0]
    tap_count = corr_table.shape[1]
    padded = jnp.pad(corr_table, ((0, 0), (0, 0), (0, tap_count)))
    flat_view = padded.reshape(groups, 3 * tap_count * tap_count)
    flat_view = jnp.pad(flat_view, ((0, 0), (0, tap_count)))
    skewed = flat_view.reshape(groups, tap_count, 3 * tap_count + 1)
    diag_sums = jnp.sum(skewed, axis=1)
    return diag_sums[:, 1 : tap_count + 1][:, ::-1]


def to_heads(rows_in):
    return rows_in.reshape(rows_in.shape[0], HEADS, HDIM).transpose(1, 0, 2)


def from_heads(pieces):
    return pieces.transpose(1, 0, 2).reshape(pieces.shape[1], HEADS * HDIM)


def gather_keys(kv_own):
    rows = kv_own.shape[1]
    wide = jnp.stack([kv_own, swap(kv_own, "xb")])
    both = jnp.stack([wide, swap(wide, "c")])
    both = both.reshape(2, 2, 2, 4, rows, 2 * HDIM).transpose(2, 0, 1, 3, 4, 5)
    return both.reshape(32 * rows, 2 * HDIM)


def scatter_keys(grad_kv, rows):
    parts = grad_kv.reshape(2, 2, 2, 4, rows, 2 * HDIM)
    parts = parts[:, 0] + swap(parts[:, 1].astype(jnp.bfloat16), "c").astype(jnp.float32)
    parts = parts[:, 0] + swap(parts[:, 1].astype(jnp.bfloat16), "xb").astype(jnp.float32)
    return parts.reshape(8, rows, 2 * HDIM).astype(jnp.bfloat16)


def weight_sum(attention, grad_residual):
    core = lax.axis_index("c")
    zl = lax.axis_index("zl")
    half = AD // 2
    mine = jnp.where(core == 0, attention[:, :half], attention[:, half:])
    theirs = jnp.where(core == 0, attention[:, half:], attention[:, :half])
    rows_a = jnp.concatenate([mine, swap(theirs, "c")], axis=0)
    rows_g = jnp.concatenate([grad_residual, swap(grad_residual, "c")], axis=0)
    peers = lax.axis_size("y")
    width = half // peers
    pieces = jnp.stack(
        [
            lax.dot_general(
                rows_g,
                rows_a[:, i * width : (i + 1) * width],
                (((0,), (0,)), ((), ())),
                preferred_element_type=jnp.float32,
            ).astype(jnp.bfloat16)
            for i in range(peers)
        ]
    )
    total = jnp.sum(exchange(pieces, "y").astype(jnp.float32), axis=0).astype(jnp.bfloat16)
    total = total.reshape(16, 2, D // 32, width)
    halves = (total[:, 0], total[:, 1])
    received = []
    for flip in range(2):
        piece = jnp.where(zl == 0, halves[flip], halves[1 - flip])
        pairs = [(a * 2 + b, b * 2 + (a ^ flip)) for a in range(2) for b in range(2)]
        received.append(lax.ppermute(piece, ("zl", "c"), pairs).astype(jnp.float32))
    total = (received[0] + received[1]).astype(jnp.bfloat16)
    total = exchange(total, ("xa", "xb", "zh"))
    return jnp.sum(total.astype(jnp.float32), axis=0).T


def local(
    query_in,
    key_in,
    value_in,
    residual,
    w_out,
    norm_gain,
    short_taps,
    filters,
    skip_gain,
    cotangent,
):
    tok_rows = query_in.shape[1]
    score_scale = HDIM ** (-0.5)
    xb = lax.axis_index("xb")
    core = lax.axis_index("c")

    kv_send = jnp.concatenate([to_heads(key_in[0]), to_heads(value_in[0])], axis=2)
    kv_own = exchange(kv_send, HEAD_AXES)
    query_rows = exchange(to_heads(query_in[0]), HEAD_AXES).reshape(8 * tok_rows, HDIM)
    kv_all = gather_keys(kv_own)
    keys_all = kv_all[:, :HDIM]
    values_all = kv_all[:, HDIM:]
    query_total = 8 * tok_rows
    seq_len = 32 * tok_rows
    q_index = jnp.arange(query_total, dtype=jnp.int32)
    q_block = q_index // tok_rows
    q_pos = (((q_block // 4) * 2 + xb) * 4 + q_block % 4) * 2 + core
    q_pos = q_pos * tok_rows + q_index % tok_rows
    k_index = jnp.arange(seq_len, dtype=jnp.int32)
    k_block = k_index // tok_rows
    k_xa, k_cr, k_xr, k_zh = k_block // 16, k_block // 8 % 2, k_block // 4 % 2, k_block % 4
    k_pos = ((k_xa * 2 + (xb ^ k_xr)) * 4 + k_zh) * 2 + (core ^ k_cr)
    k_pos = k_pos * tok_rows + k_index % tok_rows
    block_len = query_total // 2
    block_spans = [(0, seq_len // 2), (block_len, seq_len)]
    out_blocks = []
    kept_probs = []
    for first_row, key_limit in block_spans:
        logits = (
            jnp.einsum(
                "qd,kd->qk",
                query_rows[first_row : first_row + block_len],
                keys_all[:key_limit],
                preferred_element_type=jnp.float32,
            )
            * score_scale
        )
        allowed = q_pos[first_row : first_row + block_len, None] >= k_pos[None, :key_limit]
        logits = jnp.where(allowed, logits, -jnp.inf)
        row_max = jnp.max(logits, axis=-1, keepdims=True)
        log_total = row_max + jnp.log(jnp.sum(jnp.exp(logits - row_max), axis=-1, keepdims=True))
        probs = jnp.exp(logits - log_total)
        probs_low = probs.astype(jnp.bfloat16)
        out_blocks.append(
            jnp.dot(probs_low, values_all[:key_limit], preferred_element_type=jnp.float32).astype(
                jnp.bfloat16
            )
        )
        kept_probs.append(probs)
    head_out = jnp.concatenate(out_blocks, axis=0)
    attention = from_heads(exchange(head_out.reshape(8, tok_rows, HDIM), HEAD_AXES))
    x_float = residual[0].astype(jnp.float32) + jnp.dot(
        attention, w_out, preferred_element_type=jnp.float32
    )
    x_first = lax.optimization_barrier(x_float.astype(jnp.bfloat16))
    x_float = x_first.astype(jnp.float32)
    inv_rms = lax.rsqrt(jnp.mean(x_float * x_float, axis=-1, keepdims=True) + 1e-05)
    normed = lax.optimization_barrier((x_float * inv_rms * norm_gain).astype(jnp.bfloat16))
    prev_normed = from_behind(normed[tok_rows - (SHORT - 1) :], 1)
    normed_ext = jnp.concatenate([prev_normed, normed], axis=0).astype(jnp.float32)
    streams = jnp.zeros((3, tok_rows, D), jnp.float32)
    for tap_index in range(SHORT):
        streams = (
            streams
            + short_taps[:, tap_index, None, :]
            * normed_ext[None, SHORT - 1 - tap_index : SHORT - 1 - tap_index + tok_rows]
        )
    product = lax.optimization_barrier((streams[1] * streams[2]).astype(jnp.bfloat16))
    prev_product = from_behind(product[tok_rows - (LONG - 1) :], 1)
    blocks = tok_rows // LONG + 1
    prod_ext = jnp.concatenate([jnp.zeros((1, D), jnp.bfloat16), prev_product, product], axis=0)
    prod_blocks = prod_ext.reshape(blocks, LONG, FILTERS, FCH)
    matrix = long_matrix(filters)
    prev_part = matrix[:, :, :LONG]
    cur_part = matrix[:, :, LONG:]
    conv_out = jnp.einsum(
        "gij,bjgc->bigc", prev_part, prod_blocks[:-1], preferred_element_type=jnp.float32
    )
    conv_out = conv_out + jnp.einsum(
        "gij,bjgc->bigc", cur_part, prod_blocks[1:], preferred_element_type=jnp.float32
    )
    mixed_out = conv_out.reshape(tok_rows, D) + skip_gain * product.astype(jnp.float32)
    layer_out = (x_float + streams[0] * mixed_out).astype(jnp.bfloat16)
    grad_out = cotangent[0].astype(jnp.float32)
    grad_first = grad_out * mixed_out
    grad_mixed = lax.optimization_barrier((grad_out * streams[0]).astype(jnp.bfloat16))
    next_mixed = from_behind(grad_mixed[: LONG - 1], -1)
    mix_ext = jnp.concatenate([grad_mixed, next_mixed, jnp.zeros((1, D), jnp.bfloat16)], axis=0)
    mix_blocks = mix_ext.reshape(blocks, LONG, FILTERS, FCH)
    grad_conv = jnp.einsum(
        "gji,bjgc->bigc", cur_part, mix_blocks[:-1], preferred_element_type=jnp.float32
    )
    grad_conv = grad_conv + jnp.einsum(
        "gji,bjgc->bigc", prev_part, mix_blocks[1:], preferred_element_type=jnp.float32
    )
    grad_product = grad_conv.reshape(tok_rows, D) + skip_gain * grad_mixed.astype(jnp.float32)
    grad_skip = jnp.sum(grad_mixed.astype(jnp.float32) * product.astype(jnp.float32), axis=0)
    window = jnp.concatenate([prod_blocks[:-1], prod_blocks[1:]], axis=1)
    corr_table = jnp.einsum(
        "bigc,bjgc->gij", mix_blocks[:-1], window, preferred_element_type=jnp.float32
    )
    grad_filters = diagonal_sums(corr_table)
    grad_streams = jnp.stack([grad_first, grad_product * streams[2], grad_product * streams[1]])
    next_streams = from_behind(grad_streams[:, : SHORT - 1].astype(jnp.bfloat16), -1).astype(
        jnp.float32
    )
    stream_ext = jnp.concatenate([grad_streams, next_streams], axis=1)
    grad_normed = jnp.zeros((tok_rows, D), jnp.float32)
    tap_grads = []
    for tap_index in range(SHORT):
        grad_normed = grad_normed + jnp.sum(
            short_taps[:, tap_index, None, :] * stream_ext[:, tap_index : tap_index + tok_rows],
            axis=0,
        )
        tap_grads.append(
            jnp.sum(
                grad_streams
                * normed_ext[None, SHORT - 1 - tap_index : SHORT - 1 - tap_index + tok_rows],
                axis=1,
            )
        )
    grad_taps = jnp.stack(tap_grads).transpose(1, 0, 2)
    scaled = grad_normed * norm_gain
    grad_gain = jnp.sum(grad_normed * x_float * inv_rms, axis=0)
    grad_x = grad_out + inv_rms * (
        scaled - x_float * inv_rms * inv_rms * jnp.mean(scaled * x_float, axis=-1, keepdims=True)
    )
    grad_residual = grad_x.astype(jnp.bfloat16)
    small = jnp.concatenate(
        [
            grad_taps.reshape(3 * SHORT, D),
            grad_gain[None],
            grad_skip[None],
            grad_filters.reshape(1, FILTERS * LONG),
        ]
    )

    grad_attention = jnp.einsum(
        "td,ad->ta", grad_residual, w_out, preferred_element_type=jnp.float32
    ).astype(jnp.bfloat16)
    small_rows = small.shape[0] * D // 8 // HDIM
    fill_rows = -small_rows % 16
    small_send = small.reshape(8, small_rows, HDIM).astype(jnp.bfloat16)
    small_send = jnp.pad(small_send, ((0, 0), (0, fill_rows), (0, 0)))
    grad_recv = exchange(
        jnp.concatenate([to_heads(grad_attention), small_send], axis=1), HEAD_AXES
    )
    grad_rows_all = grad_recv[:, :tok_rows].reshape(query_total, HDIM)
    small_part = jnp.sum(grad_recv[:, tok_rows:].astype(jnp.float32), axis=0)
    slot_peers = lax.axis_size(SLOT_AXES)
    small_part = exchange(
        jnp.broadcast_to(small_part[None], (slot_peers,) + small_part.shape), SLOT_AXES
    )
    small_part = jnp.sum(small_part, axis=0)
    small_high = small_part.astype(jnp.bfloat16)
    small_low = (small_part - small_high.astype(jnp.float32)).astype(jnp.bfloat16)
    small_pair = jnp.concatenate([small_high, small_low], axis=1)

    grad_weight = weight_sum(attention, grad_residual)

    grad_kv = jnp.zeros((seq_len, 2 * HDIM), jnp.float32)
    dq_blocks = []
    for span_index, (first_row, key_limit) in enumerate(block_spans):
        probs = kept_probs[span_index]
        probs_low = probs.astype(jnp.bfloat16)
        grad_block = grad_rows_all[first_row : first_row + block_len]
        query_block = query_rows[first_row : first_row + block_len]
        grad_probs = jnp.einsum(
            "qd,kd->qk", grad_block, values_all[:key_limit], preferred_element_type=jnp.float32
        )
        row_delta = jnp.sum(
            grad_block.astype(jnp.float32)
            * head_out[first_row : first_row + block_len].astype(jnp.float32),
            axis=-1,
            keepdims=True,
        )
        grad_logits = (probs * (grad_probs - row_delta)).astype(jnp.bfloat16)
        dq_blocks.append(
            jnp.dot(grad_logits, keys_all[:key_limit], preferred_element_type=jnp.float32)
            * score_scale
        )
        grad_keys = (
            jnp.einsum("qk,qd->kd", grad_logits, query_block, preferred_element_type=jnp.float32)
            * score_scale
        )
        grad_values = jnp.einsum(
            "qk,qd->kd", probs_low, grad_block, preferred_element_type=jnp.float32
        )
        grad_kv = grad_kv.at[:key_limit].add(jnp.concatenate([grad_keys, grad_values], axis=1))
    dq_send = jnp.concatenate(dq_blocks, axis=0).reshape(8, tok_rows, HDIM).astype(jnp.bfloat16)
    grad_query = from_heads(exchange(dq_send, HEAD_AXES))
    dkv_send = jnp.concatenate(
        [
            scatter_keys(grad_kv, tok_rows),
            jnp.broadcast_to(small_pair[None], (8,) + small_pair.shape),
        ],
        axis=1,
    )
    dkv_back = exchange(dkv_send, HEAD_AXES)
    grad_key = from_heads(dkv_back[:, :tok_rows, :HDIM])
    grad_value = from_heads(dkv_back[:, :tok_rows, HDIM:])
    small_back = dkv_back[:, tok_rows : tok_rows + small_rows].astype(jnp.float32)
    small_back = (small_back[:, :, :HDIM] + small_back[:, :, HDIM:]).reshape(-1, D)
    return (
        layer_out[None],
        grad_residual[None],
        grad_query[None],
        grad_key[None],
        grad_value[None],
        grad_weight,
        small_back[3 * SHORT],
        small_back[: 3 * SHORT].reshape(3, SHORT, D),
        small_back[3 * SHORT + 2].reshape(FILTERS, LONG),
        small_back[3 * SHORT + 1],
    )


def solution(mesh):
    sequences = mesh.shape["dp"]
    split = Mesh(
        mesh.devices.reshape(2, sequences // 2, 2, 2, 4, 2), DP_AXES + CTX_AXES
    )
    rows = P(DP_AXES, CTX_AXES, None)
    in_specs = (rows, rows, rows, rows, P(), P(), P(), P(), P(), rows)
    out_specs = (rows, rows, rows, rows, rows, P(DP_AXES, CTX_AXES), P(), P(), P(), P())
    return jax.shard_map(local, mesh=split, in_specs=in_specs, out_specs=out_specs, check_vma=False)
```

```python
import jax
import jax.numpy as jnp
from jax import lax
from jax.experimental import pallas as pl
from jax.experimental.pallas import tpu as pltpu
from jax.sharding import Mesh, PartitionSpec as P

D = 1920
HEADS = 8
HDIM = 128
SHORT = 7
LONG = 128
FCH = 128
FILTERS = 15
AD = HEADS * HDIM
FAR = 16
SMALL = 3 * SHORT + 3
CHUNK = 16

DP_AXES = ("zl", "y")
CTX_AXES = ("xa", "xb", "zh", "c")
HEAD_AXES = ("xa", "zh")


def from_behind(x, by):
    peers = lax.axis_size(CTX_AXES)
    pairs = [(i, i + by) for i in range(peers) if 0 <= i + by < peers]
    return lax.ppermute(x, CTX_AXES, pairs)


def swap(x, axis):
    return lax.ppermute(x, axis, [(0, 1), (1, 0)])


def exchange(x, axes):
    return lax.all_to_all(x, axes, split_axis=0, concat_axis=0, tiled=True)


def long_matrix(filters):
    tap_count = filters.shape[1]
    groups = filters.shape[0]
    zero_fill = jnp.zeros((groups, tap_count), filters.dtype)
    reversed_taps = jnp.concatenate([zero_fill, filters[:, ::-1], zero_fill], axis=1)
    tiled = jnp.tile(reversed_taps, (1, tap_count))
    tiled = tiled[:, : tap_count * (3 * tap_count - 1)].reshape(
        groups, tap_count, 3 * tap_count - 1
    )
    return tiled[:, :, tap_count - 1 : 3 * tap_count - 1]


def hyena_kernel(
    prev_far,
    prev,
    own,
    following,
    following_far,
    x_all,
    cot_all,
    cot_next,
    cot_far,
    inv_rms,
    taps,
    gain,
    skip,
    forward_matrix,
    backward_matrix,
    layer_out,
    grad_residual,
    small,
    ext,
    cot_ext,
    prod,
    mix,
    stream,
    mixed,
    grad_prod,
    grad_stream,
    scaled_all,
    row_sum,
    reversed_sums,
):
    group = pl.program_id(0)
    groups = pl.num_programs(0)
    f32 = jnp.float32
    low = jnp.bfloat16
    edge = LONG + FAR
    columns = pl.ds(pl.multiple_of(group * FCH, FCH), FCH)

    @pl.when(group == 0)
    def _():
        prod[LONG + edge :, :] = jnp.zeros((LONG - FAR, FCH), low)
        mix[2 * LONG + FAR :, :] = jnp.zeros((LONG - FAR, FCH), low)
        row_sum[...] = jnp.zeros_like(row_sum)
        reversed_sums[...] = jnp.zeros_like(reversed_sums)
        small[groups] = jnp.zeros((SMALL, FCH), f32)

    ext[0:FAR, :] = prev_far[...].astype(f32)
    ext[FAR:edge, :] = prev[...].astype(f32)
    ext[edge : edge + LONG, :] = own[...].astype(f32)
    ext[edge + LONG : edge + 2 * LONG, :] = following[...].astype(f32)
    ext[edge + 2 * LONG :, :] = following_far[...].astype(f32)
    cot_ext[0:LONG, :] = cot_all[:, columns].astype(f32)
    cot_ext[LONG : 2 * LONG, :] = cot_next[...].astype(f32)
    cot_ext[2 * LONG :, :] = cot_far[...].astype(f32)

    for first in range(-LONG, 2 * LONG + FAR, CHUNK):
        kinds = []
        if first >= 0:
            kinds.append(0)
        if first < edge:
            kinds += [1, 2]
        sums = {}
        for tap in range(SHORT):
            rows = ext[edge + first - tap : edge + first - tap + CHUNK, :]
            for kind in kinds:
                term = taps[kind * SHORT + tap : kind * SHORT + tap + 1, :] * rows
                sums[kind] = term if tap == 0 else sums[kind] + term
        if 1 in sums:
            prod[LONG + first : LONG + first + CHUNK, :] = (sums[1] * sums[2]).astype(low)
        if 0 in sums:
            mix[first : first + CHUNK, :] = (cot_ext[first : first + CHUNK, :] * sums[0]).astype(
                low
            )
        if 0 <= first < edge:
            for kind in range(3):
                stream[kind, first : first + CHUNK, :] = sums[kind]

    def product_of(matrix, rows):
        return jnp.dot(matrix, rows, preferred_element_type=f32)

    mixed[0:LONG, :] = product_of(forward_matrix[0], prod[0 : 2 * LONG, :])
    mixed[LONG:, :] = product_of(forward_matrix[0, 0:FAR, :], prod[LONG:, :])
    grad_prod[0:LONG, :] = product_of(backward_matrix[0], mix[0 : 2 * LONG, :])
    grad_prod[LONG:, :] = product_of(backward_matrix[0, 0:FAR, :], mix[LONG:, :])
    table = lax.dot_general(
        mix[0:LONG, :], prod[0 : 2 * LONG, :], (((1,), (1,)), ((), ())), preferred_element_type=f32
    )
    row_index = lax.broadcasted_iota(jnp.int32, table.shape, 0)
    step = 1
    while step < LONG:
        moved = pltpu.roll(table, 2 * LONG - step, 1)
        table = jnp.where((row_index & step) != 0, moved, table)
        step *= 2
    diagonals = jnp.sum(table, axis=0, keepdims=True)
    diagonals = pltpu.roll(diagonals, 2 * LONG - 1, 1)[:, 0:LONG]
    reversed_sums[pl.ds(group, 1), :] = diagonals

    skip_row = skip[...]
    skip_sum = jnp.zeros((8, FCH), f32)
    for first in range(0, edge, CHUNK):
        rows = slice(first, first + CHUNK)
        prod_rows = prod[LONG + first : LONG + first + CHUNK, :].astype(f32)
        mix_rows = mix[rows, :].astype(f32)
        mixed_rows = mixed[rows, :] + skip_row * prod_rows
        grad_rows = grad_prod[rows, :] + skip_row * mix_rows
        grad_stream[0, rows, :] = cot_ext[rows, :] * mixed_rows
        grad_stream[1, rows, :] = grad_rows * stream[2, rows, :]
        grad_stream[2, rows, :] = grad_rows * stream[1, rows, :]
        if first < LONG:
            x_rows = x_all[rows, columns].astype(f32)
            layer_out[rows, :] = (x_rows + stream[0, rows, :] * mixed_rows).astype(low)
            skip_sum = skip_sum + jnp.sum((mix_rows * prod_rows).reshape(-1, 8, FCH), axis=0)

    gain_row = gain[...]
    gain_sum = jnp.zeros((8, FCH), f32)
    tap_sums = [None] * (3 * SHORT)
    for first in range(0, LONG, CHUNK):
        rows = slice(first, first + CHUNK)
        grad_normed = None
        for tap in range(SHORT):
            normed_rows = ext[edge + first - tap : edge + first - tap + CHUNK, :]
            for kind in range(3):
                at = kind * SHORT + tap
                term = taps[at : at + 1, :] * grad_stream[kind, first + tap : first + tap + CHUNK, :]
                grad_normed = term if grad_normed is None else grad_normed + term
                part = jnp.sum(
                    (grad_stream[kind, rows, :] * normed_rows).reshape(-1, 8, FCH), axis=0
                )
                tap_sums[at] = part if first == 0 else tap_sums[at] + part
        x_rows = x_all[rows, columns].astype(f32)
        scaled = grad_normed * gain_row
        scaled_all[group, rows, :] = scaled
        row_sum[rows, :] = row_sum[rows, :] + scaled * x_rows
        gain_sum = gain_sum + jnp.sum(
            (grad_normed * x_rows * inv_rms[rows, :]).reshape(-1, 8, FCH), axis=0
        )
    for at in range(3 * SHORT):
        small[group, at : at + 1, :] = jnp.sum(tap_sums[at], axis=0, keepdims=True)
    small[group, 3 * SHORT : 3 * SHORT + 1, :] = jnp.sum(gain_sum, axis=0, keepdims=True)
    small[group, 3 * SHORT + 1 : 3 * SHORT + 2, :] = jnp.sum(skip_sum, axis=0, keepdims=True)

    @pl.when(group == groups - 1)
    def _():
        turn = (
            lax.broadcasted_iota(jnp.int32, (LONG, LONG), 0)
            + lax.broadcasted_iota(jnp.int32, (LONG, LONG), 1)
            == LONG - 1
        ).astype(f32)
        filter_sums = jnp.dot(
            reversed_sums[...], turn, precision=lax.Precision.HIGHEST, preferred_element_type=f32
        )
        for g in range(FILTERS):
            small[g, SMALL - 1 : SMALL, :] = filter_sums[g : g + 1, :]
        scale = inv_rms[...]
        mean = jnp.sum(row_sum[...], axis=1, keepdims=True) * (1.0 / D)
        factor = scale * scale * mean
        for g in range(FILTERS):
            cols = slice(g * FCH, (g + 1) * FCH)
            x_cols = x_all[:, cols].astype(f32)
            grad = cot_all[:, cols].astype(f32) + scale * (scaled_all[g] - x_cols * factor)
            grad_residual[:, cols] = grad.astype(low)


def hyena(normed, sides, x_first, cotangent, cot_sides, inv_rms, taps, gain, skip, matrix):
    rows = x_first.shape[0]
    back = jnp.concatenate(
        [matrix[:, :, LONG:].transpose(0, 2, 1), matrix[:, :, :LONG].transpose(0, 2, 1)], axis=2
    )
    f32 = jnp.float32

    def part(count):
        return pl.BlockSpec((count, FCH), lambda g: (0, g))

    def whole(shape):
        return pl.BlockSpec(shape, lambda g: (0,) * len(shape))

    per_group = pl.BlockSpec((1, LONG, 2 * LONG), lambda g: (g, 0, 0))
    edge = LONG + FAR
    return pl.pallas_call(
        hyena_kernel,
        grid=(FILTERS,),
        in_specs=[
            part(FAR),
            part(rows),
            part(rows),
            part(rows),
            part(FAR),
            whole((rows, D)),
            whole((rows, D)),
            part(rows),
            part(FAR),
            whole((rows, 1)),
            part(3 * SHORT),
            part(1),
            part(1),
            per_group,
            per_group,
        ],
        out_specs=[
            part(rows),
            whole((rows, D)),
            whole((FILTERS + 1, SMALL, FCH)),
        ],
        out_shape=[
            jax.ShapeDtypeStruct((rows, D), jnp.bfloat16),
            jax.ShapeDtypeStruct((rows, D), jnp.bfloat16),
            jax.ShapeDtypeStruct((FILTERS + 1, SMALL, FCH), f32),
        ],
        scratch_shapes=[
            pltpu.VMEM((3 * LONG + 2 * FAR, FCH), f32),
            pltpu.VMEM((2 * LONG + FAR, FCH), f32),
            pltpu.VMEM((3 * LONG, FCH), jnp.bfloat16),
            pltpu.VMEM((3 * LONG, FCH), jnp.bfloat16),
            pltpu.VMEM((3, edge, FCH), f32),
            pltpu.VMEM((edge, FCH), f32),
            pltpu.VMEM((edge, FCH), f32),
            pltpu.VMEM((3, edge, FCH), f32),
            pltpu.VMEM((FILTERS, LONG, FCH), f32),
            pltpu.VMEM((LONG, FCH), f32),
            pltpu.VMEM((FILTERS + 1, FCH), f32),
        ],
        compiler_params=pltpu.CompilerParams(
            dimension_semantics=("arbitrary",), vmem_limit_bytes=32 * 1024 * 1024
        ),
        cost_estimate=pl.CostEstimate(
            flops=2 * 4 * 1024 * 1024 * 60, bytes_accessed=12 * 1024 * 1024, transcendentals=0
        ),
    )(
        sides[0],
        sides[1],
        normed,
        sides[2],
        sides[3],
        x_first,
        cotangent,
        cot_sides[0],
        cot_sides[1],
        inv_rms,
        taps.reshape(3 * SHORT, D),
        gain.reshape(1, D),
        skip.reshape(1, D),
        matrix,
        back,
    )


def to_heads(rows_in):
    return rows_in.reshape(rows_in.shape[0], HEADS, HDIM).transpose(1, 0, 2)


def from_heads(pieces):
    return pieces.transpose(1, 0, 2).reshape(pieces.shape[1], HEADS * HDIM)


def gather_keys(kv_own):
    rows = kv_own.shape[1]
    wide = jnp.stack([kv_own, swap(kv_own, "xb")])
    both = jnp.stack([wide, swap(wide, "c")])
    both = both.reshape(2, 2, 2, 4, rows, 2 * HDIM).transpose(2, 0, 1, 3, 4, 5)
    return both.reshape(32 * rows, 2 * HDIM)


def scatter_keys(grad_kv, rows):
    parts = grad_kv.reshape(2, 2, 2, 4, rows, 2 * HDIM)
    parts = parts[:, 0] + swap(parts[:, 1].astype(jnp.bfloat16), "c").astype(jnp.float32)
    parts = parts[:, 0] + swap(parts[:, 1].astype(jnp.bfloat16), "xb").astype(jnp.float32)
    return parts.reshape(8, rows, 2 * HDIM).astype(jnp.bfloat16)


def weight_sum(attention, grad_residual):
    core = lax.axis_index("c")
    zl = lax.axis_index("zl")
    half = AD // 2
    mine = jnp.where(core == 0, attention[:, :half], attention[:, half:])
    theirs = jnp.where(core == 0, attention[:, half:], attention[:, :half])
    rows_a = jnp.concatenate([mine, swap(theirs, "c")], axis=0)
    rows_g = jnp.concatenate([grad_residual, swap(grad_residual, "c")], axis=0)
    peers = lax.axis_size("y")
    width = half // peers
    pieces = jnp.stack(
        [
            lax.dot_general(
                rows_g,
                rows_a[:, i * width : (i + 1) * width],
                (((0,), (0,)), ((), ())),
                preferred_element_type=jnp.float32,
            ).astype(jnp.bfloat16)
            for i in range(peers)
        ]
    )
    total = jnp.sum(exchange(pieces, "y").astype(jnp.float32), axis=0).astype(jnp.bfloat16)
    total = total.reshape(16, 2, D // 32, width)
    halves = (total[:, 0], total[:, 1])
    received = []
    for flip in range(2):
        piece = jnp.where(zl == 0, halves[flip], halves[1 - flip])
        pairs = [(a * 2 + b, b * 2 + (a ^ flip)) for a in range(2) for b in range(2)]
        received.append(lax.ppermute(piece, ("zl", "c"), pairs).astype(jnp.float32))
    total = (received[0] + received[1]).astype(jnp.bfloat16)
    xb = lax.axis_index("xb")
    total = total.reshape(2, 2, 4, D // 32, width)
    mine = jnp.where(xb == 0, total[:, 0], total[:, 1]).astype(jnp.float32)
    theirs = jnp.where(xb == 0, total[:, 1], total[:, 0])
    total = mine + swap(theirs, "xb").astype(jnp.float32)
    return total.astype(jnp.bfloat16).reshape(8, D // 32, width)


def local(
    query_in,
    key_in,
    value_in,
    residual,
    w_out,
    norm_gain,
    short_taps,
    filters,
    skip_gain,
    cotangent,
):
    tok_rows = query_in.shape[1]
    score_scale = HDIM ** (-0.5)
    xb = lax.axis_index("xb")
    core = lax.axis_index("c")

    matrix = long_matrix(filters)
    cot_sides = (from_behind(cotangent[0], -1), from_behind(cotangent[0, :FAR], -2))
    kv_send = jnp.concatenate([to_heads(key_in[0]), to_heads(value_in[0])], axis=2)
    kv_own = exchange(kv_send, HEAD_AXES)
    query_rows = exchange(to_heads(query_in[0]), HEAD_AXES).reshape(8 * tok_rows, HDIM)
    kv_all = gather_keys(kv_own)
    keys_all = kv_all[:, :HDIM]
    values_all = kv_all[:, HDIM:]
    query_total = 8 * tok_rows
    seq_len = 32 * tok_rows
    q_index = jnp.arange(query_total, dtype=jnp.int32)
    q_block = q_index // tok_rows
    q_pos = (((q_block // 4) * 2 + xb) * 4 + q_block % 4) * 2 + core
    q_pos = q_pos * tok_rows + q_index % tok_rows
    k_index = jnp.arange(seq_len, dtype=jnp.int32)
    k_block = k_index // tok_rows
    k_xa, k_cr, k_xr, k_zh = k_block // 16, k_block // 8 % 2, k_block // 4 % 2, k_block % 4
    k_pos = ((k_xa * 2 + (xb ^ k_xr)) * 4 + k_zh) * 2 + (core ^ k_cr)
    k_pos = k_pos * tok_rows + k_index % tok_rows
    block_len = query_total // 2
    block_spans = [(0, seq_len // 2), (block_len, seq_len)]
    out_blocks = []
    kept_probs = []
    for first_row, key_limit in block_spans:
        logits = (
            jnp.einsum(
                "qd,kd->qk",
                query_rows[first_row : first_row + block_len],
                keys_all[:key_limit],
                preferred_element_type=jnp.float32,
            )
            * score_scale
        )
        allowed = q_pos[first_row : first_row + block_len, None] >= k_pos[None, :key_limit]
        logits = jnp.where(allowed, logits, -jnp.inf)
        row_max = jnp.max(logits, axis=-1, keepdims=True)
        log_total = row_max + jnp.log(jnp.sum(jnp.exp(logits - row_max), axis=-1, keepdims=True))
        probs = jnp.exp(logits - log_total)
        probs_low = probs.astype(jnp.bfloat16)
        out_blocks.append(
            jnp.dot(probs_low, values_all[:key_limit], preferred_element_type=jnp.float32).astype(
                jnp.bfloat16
            )
        )
        kept_probs.append(probs)
    head_out = jnp.concatenate(out_blocks, axis=0)
    attention = from_heads(exchange(head_out.reshape(8, tok_rows, HDIM), HEAD_AXES))
    x_float = residual[0].astype(jnp.float32) + jnp.dot(
        attention, w_out, preferred_element_type=jnp.float32
    )
    x_first = lax.optimization_barrier(x_float.astype(jnp.bfloat16))
    x_float = x_first.astype(jnp.float32)
    inv_rms = lax.rsqrt(jnp.mean(x_float * x_float, axis=-1, keepdims=True) + 1e-05)
    normed = lax.optimization_barrier((x_float * inv_rms * norm_gain).astype(jnp.bfloat16))
    sides = (
        from_behind(normed[tok_rows - FAR :], 2),
        from_behind(normed, 1),
        from_behind(normed, -1),
        from_behind(normed[:FAR], -2),
    )
    layer_out, grad_residual, small = hyena(
        normed,
        sides,
        x_first,
        cotangent[0],
        cot_sides,
        inv_rms,
        short_taps,
        norm_gain,
        skip_gain,
        matrix,
    )

    grad_attention = jnp.einsum(
        "td,ad->ta", grad_residual, w_out, preferred_element_type=jnp.float32
    ).astype(jnp.bfloat16)
    small_rows = (FILTERS + 1) * SMALL // 8
    small_send = small.reshape(8, small_rows, HDIM).astype(jnp.bfloat16)
    grad_recv = exchange(
        jnp.concatenate([to_heads(grad_attention), small_send], axis=1), HEAD_AXES
    )
    grad_rows_all = grad_recv[:, :tok_rows].reshape(query_total, HDIM)
    small_part = jnp.sum(grad_recv[:, tok_rows:].astype(jnp.float32), axis=0)
    sequences = lax.axis_size(DP_AXES)
    small_part = exchange(
        jnp.broadcast_to(small_part[None], (sequences,) + small_part.shape), DP_AXES
    )
    small_part = jnp.sum(small_part, axis=0)
    small_part = small_part + swap(small_part, "c")
    small_part = small_part + swap(small_part, "xb")
    small_high = small_part.astype(jnp.bfloat16)
    small_low = (small_part - small_high.astype(jnp.float32)).astype(jnp.bfloat16)

    weight_part = weight_sum(attention, grad_residual)

    grad_kv = jnp.zeros((seq_len, 2 * HDIM), jnp.float32)
    dq_blocks = []
    for span_index, (first_row, key_limit) in enumerate(block_spans):
        probs = kept_probs[span_index]
        probs_low = probs.astype(jnp.bfloat16)
        grad_block = grad_rows_all[first_row : first_row + block_len]
        query_block = query_rows[first_row : first_row + block_len]
        grad_probs = jnp.einsum(
            "qd,kd->qk", grad_block, values_all[:key_limit], preferred_element_type=jnp.float32
        )
        row_delta = jnp.sum(
            grad_block.astype(jnp.float32)
            * head_out[first_row : first_row + block_len].astype(jnp.float32),
            axis=-1,
            keepdims=True,
        )
        grad_logits = (probs * (grad_probs - row_delta)).astype(jnp.bfloat16)
        dq_blocks.append(
            jnp.dot(grad_logits, keys_all[:key_limit], preferred_element_type=jnp.float32)
            * score_scale
        )
        grad_keys = (
            jnp.einsum("qk,qd->kd", grad_logits, query_block, preferred_element_type=jnp.float32)
            * score_scale
        )
        grad_values = jnp.einsum(
            "qk,qd->kd", probs_low, grad_block, preferred_element_type=jnp.float32
        )
        grad_kv = grad_kv.at[:key_limit].add(jnp.concatenate([grad_keys, grad_values], axis=1))
    dq_send = jnp.concatenate(dq_blocks, axis=0).reshape(8, tok_rows, HDIM).astype(jnp.bfloat16)
    dkv = scatter_keys(grad_kv, tok_rows)
    dp_rows = weight_part.shape[2] // HDIM
    weight_rows = weight_part.shape[1] * dp_rows
    last_send = jnp.concatenate(
        [
            dq_send,
            dkv[:, :, :HDIM],
            dkv[:, :, HDIM:],
            jnp.broadcast_to(small_high[None], (8,) + small_high.shape),
            jnp.broadcast_to(small_low[None], (8,) + small_low.shape),
            weight_part.reshape(8, weight_rows, HDIM),
        ],
        axis=1,
    )
    last = exchange(last_send, HEAD_AXES)
    grad_query = from_heads(last[:, :tok_rows])
    grad_key = from_heads(last[:, tok_rows : 2 * tok_rows])
    grad_value = from_heads(last[:, 2 * tok_rows : 3 * tok_rows])
    at = 3 * tok_rows
    small_back = last[:, at : at + 2 * small_rows].astype(jnp.float32)
    small_back = small_back[:, :small_rows] + small_back[:, small_rows:]
    small_back = small_back.reshape(FILTERS + 1, SMALL, FCH)[:FILTERS].transpose(1, 0, 2)
    grad_filters = small_back[SMALL - 1]
    small_back = small_back.reshape(SMALL, D)
    grad_weight = jnp.sum(last[:, at + 2 * small_rows :].astype(jnp.float32), axis=0)
    grad_weight = grad_weight.reshape(D // 32, -1).T
    return (
        layer_out[None],
        grad_residual[None],
        grad_query[None],
        grad_key[None],
        grad_value[None],
        grad_weight,
        small_back[3 * SHORT],
        small_back[: 3 * SHORT].reshape(3, SHORT, D),
        grad_filters,
        small_back[3 * SHORT + 1],
    )


def solution(mesh):
    sequences = mesh.shape["dp"]
    split = Mesh(
        mesh.devices.reshape(2, sequences // 2, 2, 2, 4, 2), DP_AXES + CTX_AXES
    )
    rows = P(DP_AXES, CTX_AXES, None)
    in_specs = (rows, rows, rows, rows, P(), P(), P(), P(), P(), rows)
    out_specs = (rows, rows, rows, rows, rows, P(DP_AXES, CTX_AXES), P(), P(), P(), P())
    return jax.shard_map(local, mesh=split, in_specs=in_specs, out_specs=out_specs, check_vma=False)
```

```python
import jax
import jax.numpy as jnp
from jax import lax
from jax.experimental import pallas as pl
from jax.experimental.pallas import tpu as pltpu
from jax.sharding import Mesh, PartitionSpec as P

D = 1920
HEADS = 8
HDIM = 128
SHORT = 7
LONG = 128
FCH = 128
FILTERS = 15
AD = HEADS * HDIM
FAR = 16
SMALL = 3 * SHORT + 3
CHUNK = 16
SPAN = 4 * LONG

DP_AXES = ("zl", "y")
CTX_AXES = ("xa", "xb", "zh", "c")
HEAD_AXES = ("xa", "zh")


def from_behind(x, by):
    peers = lax.axis_size(CTX_AXES)
    pairs = [(i, i + by) for i in range(peers) if 0 <= i + by < peers]
    return lax.ppermute(x, CTX_AXES, pairs)


def swap(x, axis):
    return lax.ppermute(x, axis, [(0, 1), (1, 0)])


def exchange(x, axes):
    return lax.all_to_all(x, axes, split_axis=0, concat_axis=0, tiled=True)


def toeplitz_kernel(forward_rows, backward_rows, forward_matrix, backward_matrix):
    for g in range(FILTERS):
        for rows, matrix in ((forward_rows, forward_matrix), (backward_rows, backward_matrix)):
            spread = jnp.broadcast_to(rows[g : g + 1, :], (LONG, 2 * LONG))
            matrix[g] = pltpu.roll(spread, 0, 1, stride=1, stride_axis=0).astype(jnp.bfloat16)


def toeplitz(filters):
    taps = filters.astype(jnp.float32)
    gap = jnp.zeros((FILTERS, LONG), jnp.float32)
    forward_rows = jnp.concatenate([gap[:, :1], taps[:, ::-1], gap[:, 1:]], axis=1)
    backward_rows = jnp.concatenate([taps, gap], axis=1)
    shape = jax.ShapeDtypeStruct((FILTERS, LONG, 2 * LONG), jnp.bfloat16)
    return pl.pallas_call(
        toeplitz_kernel,
        out_shape=[shape, shape],
        compiler_params=pltpu.CompilerParams(vmem_limit_bytes=16 * 1024 * 1024),
        cost_estimate=pl.CostEstimate(flops=4000000, bytes_accessed=2000000, transcendentals=0),
    )(forward_rows, backward_rows)


def turn_matrix(kind):
    first = lax.broadcasted_iota(jnp.int32, (LONG, LONG), 0)
    second = lax.broadcasted_iota(jnp.int32, (LONG, LONG), 1)
    return (first + second == LONG - 1).astype(kind)


def hyena_kernel(
    prev_far,
    prev,
    own,
    following,
    following_far,
    x_all,
    cot_all,
    cot_next,
    cot_far,
    inv_rms,
    taps,
    gain,
    skip,
    forward_matrix,
    backward_matrix,
    layer_out,
    grad_residual,
    small,
    ext,
    cot_ext,
    prod,
    mix,
    stream,
    mixed,
    grad_prod,
    grad_stream,
    scaled_all,
    row_sum,
    reversed_sums,
):
    group = pl.program_id(0)
    groups = pl.num_programs(0)
    f32 = jnp.float32
    low = jnp.bfloat16
    edge = LONG + FAR
    columns = pl.ds(pl.multiple_of(group * FCH, FCH), FCH)

    @pl.when(group == 0)
    def _():
        prod[LONG + edge :, :] = jnp.zeros((LONG - FAR, FCH), low)
        mix[2 * LONG + FAR :, :] = jnp.zeros((LONG - FAR, FCH), low)
        row_sum[...] = jnp.zeros_like(row_sum)
        reversed_sums[...] = jnp.zeros_like(reversed_sums)
        small[groups] = jnp.zeros((SMALL, FCH), f32)

    ext[0:FAR, :] = prev_far[...].astype(f32)
    ext[FAR:edge, :] = prev[...].astype(f32)
    ext[edge : edge + LONG, :] = own[...].astype(f32)
    ext[edge + LONG : edge + 2 * LONG, :] = following[...].astype(f32)
    ext[edge + 2 * LONG :, :] = following_far[...].astype(f32)
    cot_ext[0:LONG, :] = cot_all[:, columns].astype(f32)
    cot_ext[LONG : 2 * LONG, :] = cot_next[...].astype(f32)
    cot_ext[2 * LONG :, :] = cot_far[...].astype(f32)

    for first in range(-LONG, 2 * LONG + FAR, CHUNK):
        kinds = []
        if first >= 0:
            kinds.append(0)
        if first < edge:
            kinds += [1, 2]
        sums = {}
        for tap in range(SHORT):
            rows = ext[edge + first - tap : edge + first - tap + CHUNK, :]
            for kind in kinds:
                term = taps[kind * SHORT + tap : kind * SHORT + tap + 1, :] * rows
                sums[kind] = term if tap == 0 else sums[kind] + term
        if 1 in sums:
            prod[LONG + first : LONG + first + CHUNK, :] = (sums[1] * sums[2]).astype(low)
        if 0 in sums:
            mix[first : first + CHUNK, :] = (cot_ext[first : first + CHUNK, :] * sums[0]).astype(
                low
            )
        if 0 <= first < edge:
            for kind in range(3):
                stream[kind, first : first + CHUNK, :] = sums[kind]

    def product_of(matrix, rows):
        return jnp.dot(matrix, rows, preferred_element_type=f32)

    mixed[0:LONG, :] = product_of(forward_matrix[0], prod[0 : 2 * LONG, :])
    mixed[LONG:, :] = product_of(forward_matrix[0, 0:FAR, :], prod[LONG:, :])
    grad_prod[0:LONG, :] = product_of(backward_matrix[0], mix[0 : 2 * LONG, :])
    grad_prod[LONG:, :] = product_of(backward_matrix[0, 0:FAR, :], mix[LONG:, :])
    turned = product_of(turn_matrix(low), mix[0:LONG, :]).astype(low)
    table = lax.dot_general(
        turned, prod[0 : 2 * LONG, :], (((1,), (1,)), ((), ())), preferred_element_type=f32
    )
    table = pltpu.roll(table, 0, 1, stride=1, stride_axis=0)
    diagonals = jnp.sum(table[:, LONG:], axis=0, keepdims=True)
    reversed_sums[pl.ds(group, 1), :] = diagonals

    skip_row = skip[...]
    skip_sum = jnp.zeros((8, FCH), f32)
    for first in range(0, edge, CHUNK):
        rows = slice(first, first + CHUNK)
        prod_rows = prod[LONG + first : LONG + first + CHUNK, :].astype(f32)
        mix_rows = mix[rows, :].astype(f32)
        mixed_rows = mixed[rows, :] + skip_row * prod_rows
        grad_rows = grad_prod[rows, :] + skip_row * mix_rows
        grad_stream[0, rows, :] = cot_ext[rows, :] * mixed_rows
        grad_stream[1, rows, :] = grad_rows * stream[2, rows, :]
        grad_stream[2, rows, :] = grad_rows * stream[1, rows, :]
        if first < LONG:
            x_rows = x_all[rows, columns].astype(f32)
            layer_out[rows, :] = (x_rows + stream[0, rows, :] * mixed_rows).astype(low)
            skip_sum = skip_sum + jnp.sum((mix_rows * prod_rows).reshape(-1, 8, FCH), axis=0)

    gain_row = gain[...]
    gain_sum = jnp.zeros((8, FCH), f32)
    tap_sums = [None] * (3 * SHORT)
    for first in range(0, LONG, CHUNK):
        rows = slice(first, first + CHUNK)
        grad_normed = None
        for tap in range(SHORT):
            normed_rows = ext[edge + first - tap : edge + first - tap + CHUNK, :]
            for kind in range(3):
                at = kind * SHORT + tap
                term = taps[at : at + 1, :] * grad_stream[kind, first + tap : first + tap + CHUNK, :]
                grad_normed = term if grad_normed is None else grad_normed + term
                part = jnp.sum(
                    (grad_stream[kind, rows, :] * normed_rows).reshape(-1, 8, FCH), axis=0
                )
                tap_sums[at] = part if first == 0 else tap_sums[at] + part
        x_rows = x_all[rows, columns].astype(f32)
        scaled = grad_normed * gain_row
        scaled_all[group, rows, :] = scaled
        row_sum[rows, :] = row_sum[rows, :] + scaled * x_rows
        gain_sum = gain_sum + jnp.sum(
            (grad_normed * x_rows * inv_rms[rows, :]).reshape(-1, 8, FCH), axis=0
        )
    for at in range(3 * SHORT):
        small[group, at : at + 1, :] = jnp.sum(tap_sums[at], axis=0, keepdims=True)
    small[group, 3 * SHORT : 3 * SHORT + 1, :] = jnp.sum(gain_sum, axis=0, keepdims=True)
    small[group, 3 * SHORT + 1 : 3 * SHORT + 2, :] = jnp.sum(skip_sum, axis=0, keepdims=True)

    @pl.when(group == groups - 1)
    def _():
        filter_sums = jnp.dot(
            reversed_sums[...], turn_matrix(f32), precision=lax.Precision.HIGHEST, preferred_element_type=f32
        )
        for g in range(FILTERS):
            small[g, SMALL - 1 : SMALL, :] = filter_sums[g : g + 1, :]
        scale = inv_rms[...]
        mean = jnp.sum(row_sum[...], axis=1, keepdims=True) * (1.0 / D)
        factor = scale * scale * mean
        for g in range(FILTERS):
            cols = slice(g * FCH, (g + 1) * FCH)
            x_cols = x_all[:, cols].astype(f32)
            grad = cot_all[:, cols].astype(f32) + scale * (scaled_all[g] - x_cols * factor)
            grad_residual[:, cols] = grad.astype(low)


def hyena(normed, sides, x_first, cotangent, cot_sides, inv_rms, taps, gain, skip, matrices):
    rows = x_first.shape[0]
    f32 = jnp.float32

    def part(count):
        return pl.BlockSpec((count, FCH), lambda g: (0, g))

    def whole(shape):
        return pl.BlockSpec(shape, lambda g: (0,) * len(shape))

    per_group = pl.BlockSpec((1, LONG, 2 * LONG), lambda g: (g, 0, 0))
    edge = LONG + FAR
    return pl.pallas_call(
        hyena_kernel,
        grid=(FILTERS,),
        in_specs=[
            part(FAR),
            part(rows),
            part(rows),
            part(rows),
            part(FAR),
            whole((rows, D)),
            whole((rows, D)),
            part(rows),
            part(FAR),
            whole((rows, 1)),
            part(3 * SHORT),
            part(1),
            part(1),
            per_group,
            per_group,
        ],
        out_specs=[
            part(rows),
            whole((rows, D)),
            whole((FILTERS + 1, SMALL, FCH)),
        ],
        out_shape=[
            jax.ShapeDtypeStruct((rows, D), jnp.bfloat16),
            jax.ShapeDtypeStruct((rows, D), jnp.bfloat16),
            jax.ShapeDtypeStruct((FILTERS + 1, SMALL, FCH), f32),
        ],
        scratch_shapes=[
            pltpu.VMEM((3 * LONG + 2 * FAR, FCH), f32),
            pltpu.VMEM((2 * LONG + FAR, FCH), f32),
            pltpu.VMEM((3 * LONG, FCH), jnp.bfloat16),
            pltpu.VMEM((3 * LONG, FCH), jnp.bfloat16),
            pltpu.VMEM((3, edge, FCH), f32),
            pltpu.VMEM((edge, FCH), f32),
            pltpu.VMEM((edge, FCH), f32),
            pltpu.VMEM((3, edge, FCH), f32),
            pltpu.VMEM((FILTERS, LONG, FCH), f32),
            pltpu.VMEM((LONG, FCH), f32),
            pltpu.VMEM((FILTERS + 1, FCH), f32),
        ],
        compiler_params=pltpu.CompilerParams(
            dimension_semantics=("arbitrary",), vmem_limit_bytes=32 * 1024 * 1024
        ),
        cost_estimate=pl.CostEstimate(
            flops=2 * 4 * 1024 * 1024 * 60, bytes_accessed=12 * 1024 * 1024, transcendentals=0
        ),
    )(
        sides[0],
        sides[1],
        normed,
        sides[2],
        sides[3],
        x_first,
        cotangent,
        cot_sides[0],
        cot_sides[1],
        inv_rms,
        taps.reshape(3 * SHORT, D),
        gain.reshape(1, D),
        skip.reshape(1, D),
        matrices[0],
        matrices[1],
    )


def allowed_keys(kind, core):
    keys = lax.broadcasted_iota(jnp.int32, (SPAN, SPAN), 0)
    queries = lax.broadcasted_iota(jnp.int32, (SPAN, SPAN), 1)
    if kind == 0:
        return queries >= keys
    return queries // LONG + core > keys // LONG


def spans_of(half):
    base = 4 * half
    spans = [(base, 0), (base + 2, 1), (base + 1, 2), (base + 3, 2)]
    return spans + [(span, 3) for span in range(base)]


def logits_of(k_rows, q_rows, kind, core):
    logits = lax.dot_general(
        k_rows, q_rows, (((1,), (1,)), ((), ())), preferred_element_type=jnp.float32
    ) * (HDIM**-0.5)
    if kind < 2:
        logits = jnp.where(allowed_keys(kind, core), logits, -jnp.inf)
    return logits


def attend_kernel(place, query, kv, out, log_total, top, total, wide):
    f32 = jnp.float32
    for half in range(2):
        q_rows = query[half * SPAN : (half + 1) * SPAN, :]
        for span, kind in spans_of(half):

            def visit(span=span, kind=kind):
                rows = slice(span * SPAN, (span + 1) * SPAN)
                logits = logits_of(kv[rows, 0:HDIM], q_rows, kind, place[1])
                high = jnp.max(logits, axis=0, keepdims=True)
                if kind > 0:
                    high = jnp.maximum(high, top[...])
                probs = jnp.exp(logits - high)
                part = jnp.sum(probs, axis=0, keepdims=True)
                values = lax.dot_general(
                    kv[rows, HDIM:],
                    probs.astype(jnp.bfloat16),
                    (((0,), (0,)), ((), ())),
                    preferred_element_type=f32,
                )
                if kind > 0:
                    shrink = jnp.exp(top[...] - high)
                    part = part + total[...] * shrink
                    values = values + wide[...] * shrink
                top[...] = high
                total[...] = part
                wide[...] = values

            if kind == 2:
                pl.when(place[0] == 1)(visit)
            else:
                visit()
        columns = slice(half * SPAN, (half + 1) * SPAN)
        out[columns, :] = (wide[...] / total[...]).T.astype(jnp.bfloat16)
        log_total[:, columns] = top[...] + jnp.log(total[...])


def attend(place, query, kv):
    count = query.shape[0]
    return pl.pallas_call(
        attend_kernel,
        in_specs=[
            pl.BlockSpec(memory_space=pltpu.SMEM),
            pl.BlockSpec(memory_space=pltpu.VMEM),
            pl.BlockSpec(memory_space=pltpu.VMEM),
        ],
        out_shape=[
            jax.ShapeDtypeStruct((count, HDIM), jnp.bfloat16),
            jax.ShapeDtypeStruct((1, count), jnp.float32),
        ],
        scratch_shapes=[
            pltpu.VMEM((1, SPAN), jnp.float32),
            pltpu.VMEM((1, SPAN), jnp.float32),
            pltpu.VMEM((HDIM, SPAN), jnp.float32),
        ],
        compiler_params=pltpu.CompilerParams(vmem_limit_bytes=32 * 1024 * 1024),
        cost_estimate=pl.CostEstimate(
            flops=1600000000, bytes_accessed=3000000, transcendentals=3000000
        ),
    )(place, query, kv)


def attend_back_kernel(
    place, query, kv, out, log_total, grad_out, grad_query, same_core, other_core, sums, wide
):
    f32 = jnp.float32
    low = jnp.bfloat16
    scale = HDIM**-0.5
    for half in range(2):
        columns = slice(half * SPAN, (half + 1) * SPAN)
        q_rows = query[columns, :]
        g_rows = grad_out[columns, :]
        both = g_rows.astype(f32) * out[columns, :].astype(f32)
        delta = jnp.sum(both.T, axis=0, keepdims=True)
        log_row = log_total[:, columns]
        for span, kind in spans_of(half):
            rows = slice(span * SPAN, (span + 1) * SPAN)
            fresh = half == 1 and span >= 4 or half == 0

            def visit(rows=rows, kind=kind, fresh=fresh):
                k_rows = kv[rows, 0:HDIM]
                logits = logits_of(k_rows, q_rows, kind, place[1])
                probs = jnp.exp(logits - log_row)
                grad_probs = lax.dot_general(
                    kv[rows, HDIM:],
                    g_rows,
                    (((1,), (1,)), ((), ())),
                    preferred_element_type=f32,
                )
                grad_logits = (probs * (grad_probs - delta)).astype(low)
                grad_k = jnp.dot(grad_logits, q_rows, preferred_element_type=f32)
                grad_v = jnp.dot(probs.astype(low), g_rows, preferred_element_type=f32)
                if fresh:
                    sums[rows, 0:HDIM] = grad_k
                    sums[rows, HDIM:] = grad_v
                else:
                    sums[rows, 0:HDIM] += grad_k
                    sums[rows, HDIM:] += grad_v
                part = lax.dot_general(
                    k_rows, grad_logits, (((0,), (0,)), ((), ())), preferred_element_type=f32
                )
                wide[...] = part if kind == 0 else wide[...] + part

            if kind == 2:
                pl.when(place[0] == 1)(visit)

                @pl.when(place[0] == 0)
                def _(rows=rows):
                    sums[rows, :] = jnp.zeros((SPAN, 2 * HDIM), f32)
            else:
                visit()
        grad_query[columns, :] = (wide[...] * scale).T.astype(low)
    for xa in range(2):
        for cr, target in ((0, same_core), (1, other_core)):
            for xr in range(2):
                span = xa * 4 + cr * 2 + xr
                rows = slice(span * SPAN, (span + 1) * SPAN)
                target[xa, xr, :, 0:HDIM] = (sums[rows, 0:HDIM] * scale).astype(low)
                target[xa, xr, :, HDIM:] = sums[rows, HDIM:].astype(low)


def attend_back(place, query, kv, out, log_total, grad_out):
    vmem = pl.BlockSpec(memory_space=pltpu.VMEM)
    part = jax.ShapeDtypeStruct((2, 2, SPAN, 2 * HDIM), jnp.bfloat16)
    return pl.pallas_call(
        attend_back_kernel,
        in_specs=[pl.BlockSpec(memory_space=pltpu.SMEM)] + [vmem] * 5,
        out_shape=[jax.ShapeDtypeStruct(query.shape, jnp.bfloat16), part, part],
        scratch_shapes=[
            pltpu.VMEM(kv.shape, jnp.float32),
            pltpu.VMEM((HDIM, SPAN), jnp.float32),
        ],
        compiler_params=pltpu.CompilerParams(vmem_limit_bytes=40 * 1024 * 1024),
        cost_estimate=pl.CostEstimate(
            flops=4000000000, bytes_accessed=6000000, transcendentals=3000000
        ),
    )(place, query, kv, out, log_total, grad_out)


def to_heads(rows_in):
    return rows_in.reshape(rows_in.shape[0], HEADS, HDIM).transpose(1, 0, 2)


def from_heads(pieces):
    return pieces.transpose(1, 0, 2).reshape(pieces.shape[1], HEADS * HDIM)


def gather_keys(kv_own):
    rows = kv_own.shape[1]
    wide = jnp.stack([kv_own, swap(kv_own, "xb")])
    both = jnp.stack([wide, swap(wide, "c")])
    both = both.reshape(2, 2, 2, 4, rows, 2 * HDIM).transpose(2, 0, 1, 3, 4, 5)
    return both.reshape(32 * rows, 2 * HDIM)


def scatter_keys(same_core, other_core):
    f32 = jnp.float32
    parts = same_core.astype(f32) + swap(other_core, "c").astype(f32)
    parts = parts[:, 0] + swap(parts[:, 1].astype(jnp.bfloat16), "xb").astype(f32)
    return parts.reshape(8, -1, 2 * HDIM).astype(jnp.bfloat16)


def weight_sum(attention, grad_residual, small_part):
    core = lax.axis_index("c")
    zl = lax.axis_index("zl")
    half = AD // 2
    mine = jnp.where(core == 0, attention[:, :half], attention[:, half:])
    theirs = jnp.where(core == 0, attention[:, half:], attention[:, :half])
    rows_a = jnp.concatenate([mine, swap(theirs, "c")], axis=0)
    rows_g = jnp.concatenate([grad_residual, swap(grad_residual, "c")], axis=0)
    peers = lax.axis_size("y")
    width = half // peers
    pieces = jnp.stack(
        [
            lax.dot_general(
                rows_g,
                rows_a[:, i * width : (i + 1) * width],
                (((0,), (0,)), ((), ())),
                preferred_element_type=jnp.float32,
            ).astype(jnp.bfloat16)
            for i in range(peers)
        ]
    )
    small_rows = small_part.reshape(1, -1, width).astype(jnp.bfloat16)
    small_rows = jnp.broadcast_to(small_rows, (peers,) + small_rows.shape[1:])
    total = exchange(jnp.concatenate([pieces, small_rows], axis=1), "y")
    total = jnp.sum(total.astype(jnp.float32), axis=0)
    small_part = total[D:]
    total = total[:D].astype(jnp.bfloat16).reshape(16, 2, D // 32, width)

    def flip(x, by):
        return lax.ppermute(x, ("zl", "c"), [(i, i ^ by) for i in range(4)])

    small_part = (small_part + flip(small_part, 2)) + (flip(small_part, 1) + flip(small_part, 3))
    small_part = small_part + swap(small_part, "xb")
    halves = (total[:, 0], total[:, 1])
    received = []
    for turn in range(2):
        piece = jnp.where(zl == 0, halves[turn], halves[1 - turn])
        pairs = [(a * 2 + b, b * 2 + (a ^ turn)) for a in range(2) for b in range(2)]
        received.append(lax.ppermute(piece, ("zl", "c"), pairs).astype(jnp.float32))
    total = (received[0] + received[1]).astype(jnp.bfloat16)
    xb = lax.axis_index("xb")
    total = total.reshape(2, 2, 4, D // 32, width)
    mine = jnp.where(xb == 0, total[:, 0], total[:, 1]).astype(jnp.float32)
    theirs = jnp.where(xb == 0, total[:, 1], total[:, 0])
    total = mine + swap(theirs, "xb").astype(jnp.float32)
    return total.astype(jnp.bfloat16).reshape(8, D // 32, width), small_part


def local(
    query_in,
    key_in,
    value_in,
    residual,
    w_out,
    norm_gain,
    short_taps,
    filters,
    skip_gain,
    cotangent,
):
    tok_rows = query_in.shape[1]
    matrices = toeplitz(filters)
    cot_sides = (from_behind(cotangent[0], -1), from_behind(cotangent[0, :FAR], -2))
    kv_send = jnp.concatenate([to_heads(key_in[0]), to_heads(value_in[0])], axis=2)
    kv_own = exchange(kv_send, HEAD_AXES)
    query_rows = exchange(to_heads(query_in[0]), HEAD_AXES).reshape(8 * tok_rows, HDIM)
    kv_all = gather_keys(kv_own)
    query_total = 8 * tok_rows
    place = jnp.stack([lax.axis_index("xb"), lax.axis_index("c")]).astype(jnp.int32)
    head_out, log_total = attend(place, query_rows, kv_all)
    attention = from_heads(exchange(head_out.reshape(8, tok_rows, HDIM), HEAD_AXES))
    x_float = residual[0].astype(jnp.float32) + jnp.dot(
        attention, w_out, preferred_element_type=jnp.float32
    )
    x_first = lax.optimization_barrier(x_float.astype(jnp.bfloat16))
    x_float = x_first.astype(jnp.float32)
    inv_rms = lax.rsqrt(jnp.mean(x_float * x_float, axis=-1, keepdims=True) + 1e-05)
    normed = lax.optimization_barrier((x_float * inv_rms * norm_gain).astype(jnp.bfloat16))
    sides = (
        from_behind(normed[tok_rows - FAR :], 2),
        from_behind(normed, 1),
        from_behind(normed, -1),
        from_behind(normed[:FAR], -2),
    )
    layer_out, grad_residual, small = hyena(
        normed,
        sides,
        x_first,
        cotangent[0],
        cot_sides,
        inv_rms,
        short_taps,
        norm_gain,
        skip_gain,
        matrices,
    )

    grad_attention = jnp.einsum(
        "td,ad->ta", grad_residual, w_out, preferred_element_type=jnp.float32
    ).astype(jnp.bfloat16)
    small_rows = (FILTERS + 1) * SMALL // 8
    small_send = small.reshape(8, small_rows, HDIM).astype(jnp.bfloat16)
    grad_recv = exchange(
        jnp.concatenate([to_heads(grad_attention), small_send], axis=1), HEAD_AXES
    )
    grad_rows_all = grad_recv[:, :tok_rows].reshape(query_total, HDIM)
    small_part = jnp.sum(grad_recv[:, tok_rows:].astype(jnp.float32), axis=0)
    weight_part, small_part = weight_sum(attention, grad_residual, small_part)
    small_high = small_part.reshape(-1, HDIM).astype(jnp.bfloat16)

    grad_query, same_core, other_core = attend_back(
        place, query_rows, kv_all, head_out, log_total, grad_rows_all
    )
    dq_send = grad_query.reshape(8, tok_rows, HDIM)
    dkv = scatter_keys(same_core, other_core)
    dp_rows = weight_part.shape[2] // HDIM
    weight_rows = weight_part.shape[1] * dp_rows
    last_send = jnp.concatenate(
        [
            dq_send,
            dkv[:, :, :HDIM],
            dkv[:, :, HDIM:],
            jnp.broadcast_to(small_high[None], (8,) + small_high.shape),
            weight_part.reshape(8, weight_rows, HDIM),
        ],
        axis=1,
    )
    last = exchange(last_send, HEAD_AXES)
    grad_query = from_heads(last[:, :tok_rows])
    grad_key = from_heads(last[:, tok_rows : 2 * tok_rows])
    grad_value = from_heads(last[:, 2 * tok_rows : 3 * tok_rows])
    at = 3 * tok_rows
    small_back = last[:, at : at + small_rows].astype(jnp.float32)
    small_back = small_back.reshape(FILTERS + 1, SMALL, FCH)[:FILTERS].transpose(1, 0, 2)
    grad_filters = small_back[SMALL - 1]
    small_back = small_back.reshape(SMALL, D)
    grad_weight = jnp.sum(last[:, at + small_rows :].astype(jnp.float32), axis=0)
    grad_weight = grad_weight.reshape(D // 32, -1).T
    return (
        layer_out[None],
        grad_residual[None],
        grad_query[None],
        grad_key[None],
        grad_value[None],
        grad_weight,
        small_back[3 * SHORT],
        small_back[: 3 * SHORT].reshape(3, SHORT, D),
        grad_filters,
        small_back[3 * SHORT + 1],
    )


def solution(mesh):
    sequences = mesh.shape["dp"]
    split = Mesh(
        mesh.devices.reshape(2, sequences // 2, 2, 2, 4, 2), DP_AXES + CTX_AXES
    )
    rows = P(DP_AXES, CTX_AXES, None)
    in_specs = (rows, rows, rows, rows, P(), P(), P(), P(), P(), rows)
    out_specs = (rows, rows, rows, rows, rows, P(DP_AXES, CTX_AXES), P(), P(), P(), P())
    return jax.shard_map(local, mesh=split, in_specs=in_specs, out_specs=out_specs, check_vma=False)
```

```python
import jax
import jax.numpy as jnp
from jax import lax
from jax.experimental import pallas as pl
from jax.experimental.pallas import tpu as pltpu
from jax.sharding import Mesh, PartitionSpec as P

D = 1920
HEADS = 8
HDIM = 128
SHORT = 7
LONG = 128
FCH = 128
FILTERS = 15
AD = HEADS * HDIM
FAR = 16
SMALL = 3 * SHORT + 3
CHUNK = 16
SPAN = 4 * LONG

DP_AXES = ("zl", "y")
CTX_AXES = ("xa", "xb", "zh", "c")
HEAD_AXES = ("xa", "zh")


def from_behind(x, by):
    peers = lax.axis_size(CTX_AXES)
    pairs = [(i, i + by) for i in range(peers) if 0 <= i + by < peers]
    return lax.ppermute(x, CTX_AXES, pairs)


def swap(x, axis):
    return lax.ppermute(x, axis, [(0, 1), (1, 0)])


def exchange(x, axes):
    return lax.all_to_all(x, axes, split_axis=0, concat_axis=0, tiled=True)


def toeplitz_kernel(forward_rows, backward_rows, forward_matrix, backward_matrix):
    for g in range(FILTERS):
        for rows, matrix in ((forward_rows, forward_matrix), (backward_rows, backward_matrix)):
            spread = jnp.broadcast_to(rows[g : g + 1, :], (LONG, 2 * LONG))
            matrix[g] = pltpu.roll(spread, 0, 1, stride=1, stride_axis=0).astype(jnp.bfloat16)


def toeplitz(filters):
    taps = filters.astype(jnp.float32)
    gap = jnp.zeros((FILTERS, LONG), jnp.float32)
    forward_rows = jnp.concatenate([gap[:, :1], taps[:, ::-1], gap[:, 1:]], axis=1)
    backward_rows = jnp.concatenate([taps, gap], axis=1)
    shape = jax.ShapeDtypeStruct((FILTERS, LONG, 2 * LONG), jnp.bfloat16)
    return pl.pallas_call(
        toeplitz_kernel,
        out_shape=[shape, shape],
        compiler_params=pltpu.CompilerParams(vmem_limit_bytes=16 * 1024 * 1024),
        cost_estimate=pl.CostEstimate(flops=4000000, bytes_accessed=2000000, transcendentals=0),
    )(forward_rows, backward_rows)


def turn_matrix(kind):
    first = lax.broadcasted_iota(jnp.int32, (LONG, LONG), 0)
    second = lax.broadcasted_iota(jnp.int32, (LONG, LONG), 1)
    return (first + second == LONG - 1).astype(kind)


def hyena_kernel(
    prev_far,
    prev,
    own,
    following,
    following_far,
    x_all,
    cot_all,
    cot_next,
    cot_far,
    inv_rms,
    taps,
    gain,
    skip,
    forward_matrix,
    backward_matrix,
    layer_out,
    grad_residual,
    small,
    ext,
    cot_ext,
    prod,
    mix,
    stream,
    mixed,
    grad_prod,
    grad_stream,
    scaled_all,
    row_sum,
    reversed_sums,
):
    group = pl.program_id(0)
    groups = pl.num_programs(0)
    f32 = jnp.float32
    low = jnp.bfloat16
    edge = LONG + FAR
    columns = pl.ds(pl.multiple_of(group * FCH, FCH), FCH)

    @pl.when(group == 0)
    def _():
        prod[LONG + edge :, :] = jnp.zeros((LONG - FAR, FCH), low)
        mix[2 * LONG + FAR :, :] = jnp.zeros((LONG - FAR, FCH), low)
        row_sum[...] = jnp.zeros_like(row_sum)
        reversed_sums[...] = jnp.zeros_like(reversed_sums)
        small[groups] = jnp.zeros((SMALL, FCH), f32)

    ext[0:FAR, :] = prev_far[...].astype(f32)
    ext[FAR:edge, :] = prev[...].astype(f32)
    ext[edge : edge + LONG, :] = own[...].astype(f32)
    ext[edge + LONG : edge + 2 * LONG, :] = following[...].astype(f32)
    ext[edge + 2 * LONG :, :] = following_far[...].astype(f32)
    cot_ext[0:LONG, :] = cot_all[:, columns].astype(f32)
    cot_ext[LONG : 2 * LONG, :] = cot_next[...].astype(f32)
    cot_ext[2 * LONG :, :] = cot_far[...].astype(f32)

    for first in range(-LONG, 2 * LONG + FAR, CHUNK):
        kinds = []
        if first >= 0:
            kinds.append(0)
        if first < edge:
            kinds += [1, 2]
        sums = {}
        for tap in range(SHORT):
            rows = ext[edge + first - tap : edge + first - tap + CHUNK, :]
            for kind in kinds:
                term = taps[kind * SHORT + tap : kind * SHORT + tap + 1, :] * rows
                sums[kind] = term if tap == 0 else sums[kind] + term
        if 1 in sums:
            prod[LONG + first : LONG + first + CHUNK, :] = (sums[1] * sums[2]).astype(low)
        if 0 in sums:
            mix[first : first + CHUNK, :] = (cot_ext[first : first + CHUNK, :] * sums[0]).astype(
                low
            )
        if 0 <= first < edge:
            for kind in range(3):
                stream[kind, first : first + CHUNK, :] = sums[kind]

    def product_of(matrix, rows):
        return jnp.dot(matrix, rows, preferred_element_type=f32)

    mixed[0:LONG, :] = product_of(forward_matrix[0], prod[0 : 2 * LONG, :])
    mixed[LONG:, :] = product_of(forward_matrix[0, 0:FAR, :], prod[LONG:, :])
    grad_prod[0:LONG, :] = product_of(backward_matrix[0], mix[0 : 2 * LONG, :])
    grad_prod[LONG:, :] = product_of(backward_matrix[0, 0:FAR, :], mix[LONG:, :])
    turned = product_of(turn_matrix(low), mix[0:LONG, :]).astype(low)
    table = lax.dot_general(
        turned, prod[0 : 2 * LONG, :], (((1,), (1,)), ((), ())), preferred_element_type=f32
    )
    table = pltpu.roll(table, 0, 1, stride=1, stride_axis=0)
    diagonals = jnp.sum(table[:, LONG:], axis=0, keepdims=True)
    reversed_sums[pl.ds(group, 1), :] = diagonals

    skip_row = skip[...]
    skip_sum = jnp.zeros((8, FCH), f32)
    for first in range(0, edge, CHUNK):
        rows = slice(first, first + CHUNK)
        prod_rows = prod[LONG + first : LONG + first + CHUNK, :].astype(f32)
        mix_rows = mix[rows, :].astype(f32)
        mixed_rows = mixed[rows, :] + skip_row * prod_rows
        grad_rows = grad_prod[rows, :] + skip_row * mix_rows
        grad_stream[0, rows, :] = cot_ext[rows, :] * mixed_rows
        grad_stream[1, rows, :] = grad_rows * stream[2, rows, :]
        grad_stream[2, rows, :] = grad_rows * stream[1, rows, :]
        if first < LONG:
            x_rows = x_all[rows, columns].astype(f32)
            layer_out[rows, :] = (x_rows + stream[0, rows, :] * mixed_rows).astype(low)
            skip_sum = skip_sum + jnp.sum((mix_rows * prod_rows).reshape(-1, 8, FCH), axis=0)

    gain_row = gain[...]
    gain_sum = jnp.zeros((8, FCH), f32)
    tap_sums = [None] * (3 * SHORT)
    for first in range(0, LONG, CHUNK):
        rows = slice(first, first + CHUNK)
        grad_normed = None
        for tap in range(SHORT):
            normed_rows = ext[edge + first - tap : edge + first - tap + CHUNK, :]
            for kind in range(3):
                at = kind * SHORT + tap
                term = taps[at : at + 1, :] * grad_stream[kind, first + tap : first + tap + CHUNK, :]
                grad_normed = term if grad_normed is None else grad_normed + term
                part = jnp.sum(
                    (grad_stream[kind, rows, :] * normed_rows).reshape(-1, 8, FCH), axis=0
                )
                tap_sums[at] = part if first == 0 else tap_sums[at] + part
        x_rows = x_all[rows, columns].astype(f32)
        scaled = grad_normed * gain_row
        scaled_all[group, rows, :] = scaled
        row_sum[rows, :] = row_sum[rows, :] + scaled * x_rows
        gain_sum = gain_sum + jnp.sum(
            (grad_normed * x_rows * inv_rms[rows, :]).reshape(-1, 8, FCH), axis=0
        )
    for at in range(3 * SHORT):
        small[group, at : at + 1, :] = jnp.sum(tap_sums[at], axis=0, keepdims=True)
    small[group, 3 * SHORT : 3 * SHORT + 1, :] = jnp.sum(gain_sum, axis=0, keepdims=True)
    small[group, 3 * SHORT + 1 : 3 * SHORT + 2, :] = jnp.sum(skip_sum, axis=0, keepdims=True)

    @pl.when(group == groups - 1)
    def _():
        filter_sums = jnp.dot(
            reversed_sums[...], turn_matrix(f32), precision=lax.Precision.HIGHEST, preferred_element_type=f32
        )
        for g in range(FILTERS):
            small[g, SMALL - 1 : SMALL, :] = filter_sums[g : g + 1, :]
        scale = inv_rms[...]
        mean = jnp.sum(row_sum[...], axis=1, keepdims=True) * (1.0 / D)
        factor = scale * scale * mean
        for g in range(FILTERS):
            cols = slice(g * FCH, (g + 1) * FCH)
            x_cols = x_all[:, cols].astype(f32)
            grad = cot_all[:, cols].astype(f32) + scale * (scaled_all[g] - x_cols * factor)
            grad_residual[:, cols] = grad.astype(low)


def hyena(normed, sides, x_first, cotangent, cot_sides, inv_rms, taps, gain, skip, matrices):
    rows = x_first.shape[0]
    f32 = jnp.float32

    def part(count):
        return pl.BlockSpec((count, FCH), lambda g: (0, g))

    def whole(shape):
        return pl.BlockSpec(shape, lambda g: (0,) * len(shape))

    per_group = pl.BlockSpec((1, LONG, 2 * LONG), lambda g: (g, 0, 0))
    edge = LONG + FAR
    return pl.pallas_call(
        hyena_kernel,
        grid=(FILTERS,),
        in_specs=[
            part(FAR),
            part(rows),
            part(rows),
            part(rows),
            part(FAR),
            whole((rows, D)),
            whole((rows, D)),
            part(rows),
            part(FAR),
            whole((rows, 1)),
            part(3 * SHORT),
            part(1),
            part(1),
            per_group,
            per_group,
        ],
        out_specs=[
            part(rows),
            whole((rows, D)),
            whole((FILTERS + 1, SMALL, FCH)),
        ],
        out_shape=[
            jax.ShapeDtypeStruct((rows, D), jnp.bfloat16),
            jax.ShapeDtypeStruct((rows, D), jnp.bfloat16),
            jax.ShapeDtypeStruct((FILTERS + 1, SMALL, FCH), f32),
        ],
        scratch_shapes=[
            pltpu.VMEM((3 * LONG + 2 * FAR, FCH), f32),
            pltpu.VMEM((2 * LONG + FAR, FCH), f32),
            pltpu.VMEM((3 * LONG, FCH), jnp.bfloat16),
            pltpu.VMEM((3 * LONG, FCH), jnp.bfloat16),
            pltpu.VMEM((3, edge, FCH), f32),
            pltpu.VMEM((edge, FCH), f32),
            pltpu.VMEM((edge, FCH), f32),
            pltpu.VMEM((3, edge, FCH), f32),
            pltpu.VMEM((FILTERS, LONG, FCH), f32),
            pltpu.VMEM((LONG, FCH), f32),
            pltpu.VMEM((FILTERS + 1, FCH), f32),
        ],
        compiler_params=pltpu.CompilerParams(
            dimension_semantics=("arbitrary",), vmem_limit_bytes=32 * 1024 * 1024
        ),
        cost_estimate=pl.CostEstimate(
            flops=2 * 4 * 1024 * 1024 * 60, bytes_accessed=12 * 1024 * 1024, transcendentals=0
        ),
    )(
        sides[0],
        sides[1],
        normed,
        sides[2],
        sides[3],
        x_first,
        cotangent,
        cot_sides[0],
        cot_sides[1],
        inv_rms,
        taps.reshape(3 * SHORT, D),
        gain.reshape(1, D),
        skip.reshape(1, D),
        matrices[0],
        matrices[1],
    )


def allowed_keys(kind, core):
    keys = lax.broadcasted_iota(jnp.int32, (SPAN, SPAN), 0)
    queries = lax.broadcasted_iota(jnp.int32, (SPAN, SPAN), 1)
    if kind == 0:
        return queries >= keys
    return queries // LONG + core > keys // LONG


def spans_of(half):
    base = 4 * half
    spans = [(base, 0), (base + 2, 1), (base + 1, 2), (base + 3, 2)]
    return spans + [(span, 3) for span in range(base)]


def logits_of(k_rows, q_rows, kind, core):
    logits = lax.dot_general(
        k_rows, q_rows, (((1,), (1,)), ((), ())), preferred_element_type=jnp.float32
    ) * (HDIM**-0.5)
    if kind < 2:
        logits = jnp.where(allowed_keys(kind, core), logits, -jnp.inf)
    return logits


def attend_kernel(place, query, kv, out, log_total, top, total, wide):
    f32 = jnp.float32
    for half in range(2):
        q_rows = query[half * SPAN : (half + 1) * SPAN, :]
        for span, kind in spans_of(half):

            def visit(span=span, kind=kind):
                rows = slice(span * SPAN, (span + 1) * SPAN)
                logits = logits_of(kv[rows, 0:HDIM], q_rows, kind, place[1])
                high = jnp.max(logits, axis=0, keepdims=True)
                if kind > 0:
                    high = jnp.maximum(high, top[...])
                probs = jnp.exp(logits - high)
                part = jnp.sum(probs, axis=0, keepdims=True)
                values = lax.dot_general(
                    kv[rows, HDIM:],
                    probs.astype(jnp.bfloat16),
                    (((0,), (0,)), ((), ())),
                    preferred_element_type=f32,
                )
                if kind > 0:
                    shrink = jnp.exp(top[...] - high)
                    part = part + total[...] * shrink
                    values = values + wide[...] * shrink
                top[...] = high
                total[...] = part
                wide[...] = values

            if kind == 2:
                pl.when(place[0] == 1)(visit)
            else:
                visit()
        columns = slice(half * SPAN, (half + 1) * SPAN)
        out[columns, :] = (wide[...] / total[...]).T.astype(jnp.bfloat16)
        log_total[:, columns] = top[...] + jnp.log(total[...])


def attend(place, query, kv):
    count = query.shape[0]
    return pl.pallas_call(
        attend_kernel,
        in_specs=[
            pl.BlockSpec(memory_space=pltpu.SMEM),
            pl.BlockSpec(memory_space=pltpu.VMEM),
            pl.BlockSpec(memory_space=pltpu.VMEM),
        ],
        out_shape=[
            jax.ShapeDtypeStruct((count, HDIM), jnp.bfloat16),
            jax.ShapeDtypeStruct((1, count), jnp.float32),
        ],
        scratch_shapes=[
            pltpu.VMEM((1, SPAN), jnp.float32),
            pltpu.VMEM((1, SPAN), jnp.float32),
            pltpu.VMEM((HDIM, SPAN), jnp.float32),
        ],
        compiler_params=pltpu.CompilerParams(vmem_limit_bytes=32 * 1024 * 1024),
        cost_estimate=pl.CostEstimate(
            flops=1600000000, bytes_accessed=3000000, transcendentals=3000000
        ),
    )(place, query, kv)


def attend_back_kernel(
    place, query, kv, out, log_total, grad_out, grad_query, same_core, other_core, sums, wide
):
    f32 = jnp.float32
    low = jnp.bfloat16
    scale = HDIM**-0.5
    for half in range(2):
        columns = slice(half * SPAN, (half + 1) * SPAN)
        q_rows = query[columns, :]
        g_rows = grad_out[columns, :]
        both = g_rows.astype(f32) * out[columns, :].astype(f32)
        delta = jnp.sum(both.T, axis=0, keepdims=True)
        log_row = log_total[:, columns]
        for span, kind in spans_of(half):
            rows = slice(span * SPAN, (span + 1) * SPAN)
            fresh = half == 1 and span >= 4 or half == 0

            def visit(rows=rows, kind=kind, fresh=fresh):
                k_rows = kv[rows, 0:HDIM]
                logits = logits_of(k_rows, q_rows, kind, place[1])
                probs = jnp.exp(logits - log_row)
                grad_probs = lax.dot_general(
                    kv[rows, HDIM:],
                    g_rows,
                    (((1,), (1,)), ((), ())),
                    preferred_element_type=f32,
                )
                grad_logits = (probs * (grad_probs - delta)).astype(low)
                grad_k = jnp.dot(grad_logits, q_rows, preferred_element_type=f32)
                grad_v = jnp.dot(probs.astype(low), g_rows, preferred_element_type=f32)
                if fresh:
                    sums[rows, 0:HDIM] = grad_k
                    sums[rows, HDIM:] = grad_v
                else:
                    sums[rows, 0:HDIM] += grad_k
                    sums[rows, HDIM:] += grad_v
                part = lax.dot_general(
                    k_rows, grad_logits, (((0,), (0,)), ((), ())), preferred_element_type=f32
                )
                wide[...] = part if kind == 0 else wide[...] + part

            if kind == 2:
                pl.when(place[0] == 1)(visit)

                @pl.when(place[0] == 0)
                def _(rows=rows):
                    sums[rows, :] = jnp.zeros((SPAN, 2 * HDIM), f32)
            else:
                visit()
        grad_query[columns, :] = (wide[...] * scale).T.astype(low)
    for xa in range(2):
        for cr, target in ((0, same_core), (1, other_core)):
            for xr in range(2):
                span = xa * 4 + cr * 2 + xr
                rows = slice(span * SPAN, (span + 1) * SPAN)
                target[xa, xr, :, 0:HDIM] = (sums[rows, 0:HDIM] * scale).astype(low)
                target[xa, xr, :, HDIM:] = sums[rows, HDIM:].astype(low)


def attend_back(place, query, kv, out, log_total, grad_out):
    vmem = pl.BlockSpec(memory_space=pltpu.VMEM)
    part = jax.ShapeDtypeStruct((2, 2, SPAN, 2 * HDIM), jnp.bfloat16)
    return pl.pallas_call(
        attend_back_kernel,
        in_specs=[pl.BlockSpec(memory_space=pltpu.SMEM)] + [vmem] * 5,
        out_shape=[jax.ShapeDtypeStruct(query.shape, jnp.bfloat16), part, part],
        scratch_shapes=[
            pltpu.VMEM(kv.shape, jnp.float32),
            pltpu.VMEM((HDIM, SPAN), jnp.float32),
        ],
        compiler_params=pltpu.CompilerParams(vmem_limit_bytes=40 * 1024 * 1024),
        cost_estimate=pl.CostEstimate(
            flops=4000000000, bytes_accessed=6000000, transcendentals=3000000
        ),
    )(place, query, kv, out, log_total, grad_out)


def to_heads(rows_in):
    return rows_in.reshape(rows_in.shape[0], HEADS, HDIM).transpose(1, 0, 2)


def from_heads(pieces):
    return pieces.transpose(1, 0, 2).reshape(pieces.shape[1], HEADS * HDIM)


def gather_keys(kv_own):
    wide = jnp.stack([kv_own, swap(kv_own, "xb")])
    both = jnp.stack([wide, swap(wide, "c")])
    both = both.reshape(2, 2, 2, 4, 2, -1, HDIM).transpose(2, 0, 1, 3, 5, 4, 6)
    return both.reshape(-1, 2 * HDIM)


def weight_pieces(attention, grad_residual):
    core = lax.axis_index("c")
    half = AD // 2
    mine = jnp.where(core == 0, attention[:, :half], attention[:, half:])
    theirs = jnp.where(core == 0, attention[:, half:], attention[:, :half])
    rows_a = jnp.concatenate([mine, swap(theirs, "c")], axis=0)
    rows_g = jnp.concatenate([grad_residual, swap(grad_residual, "c")], axis=0)
    peers = lax.axis_size("y")
    width = half // peers
    at = lax.axis_index("y")
    pieces = []
    for step in range(peers):
        columns = lax.dynamic_slice_in_dim(rows_a, (at + step) % peers * width, width, axis=1)
        piece = lax.dot_general(
            rows_g, columns, (((0,), (0,)), ((), ())), preferred_element_type=jnp.float32
        )
        pieces.append(piece.astype(jnp.bfloat16))
    return lax.optimization_barrier(pieces)


def weight_over_y(pieces):
    peers = len(pieces)
    total = pieces[0].astype(jnp.float32)
    for step in range(1, peers):
        pairs = [(i, (i + step) % peers) for i in range(peers)]
        total = total + lax.ppermute(pieces[step], "y", pairs).astype(jnp.float32)
    return total.astype(jnp.bfloat16)


def weight_over_zl(total):
    zl = lax.axis_index("zl")
    total = total.reshape(16, 2, D // 32, -1)
    halves = (total[:, 0], total[:, 1])
    received = []
    for turn in range(2):
        piece = jnp.where(zl == 0, halves[turn], halves[1 - turn])
        pairs = [(a * 2 + b, b * 2 + (a ^ turn)) for a in range(2) for b in range(2)]
        received.append(lax.ppermute(piece, ("zl", "c"), pairs).astype(jnp.float32))
    return (received[0] + received[1]).astype(jnp.bfloat16)


def weight_over_xb(total):
    xb = lax.axis_index("xb")
    total = total.reshape(2, 2, 4, D // 32, -1)
    mine = jnp.where(xb == 0, total[:, 0], total[:, 1]).astype(jnp.float32)
    theirs = jnp.where(xb == 0, total[:, 1], total[:, 0])
    total = mine + swap(theirs, "xb").astype(jnp.float32)
    return total.astype(jnp.bfloat16).reshape(8, D // 32, -1)


def local(
    query_in,
    key_in,
    value_in,
    residual,
    w_out,
    norm_gain,
    short_taps,
    filters,
    skip_gain,
    cotangent,
):
    tok_rows = query_in.shape[1]
    matrices = toeplitz(filters)
    cot_sides = (from_behind(cotangent[0], -1), from_behind(cotangent[0, :FAR], -2))
    qkv_send = jnp.concatenate(
        [to_heads(query_in[0]), to_heads(key_in[0]), to_heads(value_in[0])], axis=1
    )
    qkv_own = exchange(qkv_send, HEAD_AXES)
    query_rows = qkv_own[:, :tok_rows].reshape(8 * tok_rows, HDIM)
    kv_all = gather_keys(qkv_own[:, tok_rows:])
    query_total = 8 * tok_rows
    place = jnp.stack([lax.axis_index("xb"), lax.axis_index("c")]).astype(jnp.int32)
    head_out, log_total = attend(place, query_rows, kv_all)
    attention = from_heads(exchange(head_out.reshape(8, tok_rows, HDIM), HEAD_AXES))
    x_float = residual[0].astype(jnp.float32) + jnp.dot(
        attention, w_out, preferred_element_type=jnp.float32
    )
    x_first = lax.optimization_barrier(x_float.astype(jnp.bfloat16))
    x_float = x_first.astype(jnp.float32)
    inv_rms = lax.rsqrt(jnp.mean(x_float * x_float, axis=-1, keepdims=True) + 1e-05)
    normed = lax.optimization_barrier((x_float * inv_rms * norm_gain).astype(jnp.bfloat16))
    sides = (
        from_behind(normed[tok_rows - FAR :], 2),
        from_behind(normed, 1),
        from_behind(normed, -1),
        from_behind(normed[:FAR], -2),
    )
    layer_out, grad_residual, small = hyena(
        normed,
        sides,
        x_first,
        cotangent[0],
        cot_sides,
        inv_rms,
        short_taps,
        norm_gain,
        skip_gain,
        matrices,
    )

    grad_attention = jnp.einsum(
        "td,ad->ta", grad_residual, w_out, preferred_element_type=jnp.float32
    ).astype(jnp.bfloat16)
    small_rows = (FILTERS + 1) * SMALL // 8
    small_send = small.reshape(8, small_rows, HDIM).astype(jnp.bfloat16)
    grad_recv = exchange(
        jnp.concatenate([to_heads(grad_attention), small_send], axis=1), HEAD_AXES
    )
    weight_part = weight_over_y(weight_pieces(attention, grad_residual))
    grad_rows_all = grad_recv[:, :tok_rows].reshape(query_total, HDIM)
    small_part = jnp.sum(grad_recv[:, tok_rows:].astype(jnp.float32), axis=0)
    sequences = lax.axis_size(DP_AXES)
    small_part = exchange(
        jnp.broadcast_to(small_part[None], (sequences,) + small_part.shape), DP_AXES
    )
    small_part = jnp.sum(small_part, axis=0)
    small_part = small_part + swap(small_part, "c")
    small_part = small_part + swap(small_part, "xb")
    small_part = small_part.astype(jnp.bfloat16)

    grad_query, same_core, other_core = attend_back(
        place, query_rows, kv_all, head_out, log_total, grad_rows_all
    )
    dq_send = grad_query.reshape(8, tok_rows, HDIM)
    dkv = same_core.astype(jnp.float32) + swap(other_core, "c").astype(jnp.float32)
    weight_part = weight_over_zl(weight_part)
    dkv = dkv[:, 0] + swap(dkv[:, 1].astype(jnp.bfloat16), "xb").astype(jnp.float32)
    dkv = dkv.reshape(8, tok_rows, 2 * HDIM).astype(jnp.bfloat16)
    weight_part = weight_over_xb(weight_part)
    weight_rows = weight_part.size // (8 * HDIM)
    last_send = jnp.concatenate(
        [
            dq_send,
            dkv[:, :, :HDIM],
            dkv[:, :, HDIM:],
            jnp.broadcast_to(small_part[None], (8,) + small_part.shape),
            weight_part.reshape(8, weight_rows, HDIM),
        ],
        axis=1,
    )
    last = exchange(last_send, HEAD_AXES)
    grad_query = from_heads(last[:, :tok_rows])
    grad_key = from_heads(last[:, tok_rows : 2 * tok_rows])
    grad_value = from_heads(last[:, 2 * tok_rows : 3 * tok_rows])
    sums_back = last[:, 3 * tok_rows :].astype(jnp.float32)
    small_back = sums_back[:, :small_rows]
    small_back = small_back.reshape(FILTERS + 1, SMALL, FCH)[:FILTERS].transpose(1, 0, 2)
    grad_filters = small_back[SMALL - 1]
    small_back = small_back.reshape(SMALL, D)
    grad_weight = jnp.sum(sums_back[:, small_rows:], axis=0)
    grad_weight = grad_weight.reshape(D // 32, -1).T
    return (
        layer_out[None],
        grad_residual[None],
        grad_query[None],
        grad_key[None],
        grad_value[None],
        grad_weight,
        small_back[3 * SHORT],
        small_back[: 3 * SHORT].reshape(3, SHORT, D),
        grad_filters,
        small_back[3 * SHORT + 1],
    )


def solution(mesh):
    sequences = mesh.shape["dp"]
    split = Mesh(
        mesh.devices.reshape(2, sequences // 2, 2, 2, 4, 2), DP_AXES + CTX_AXES
    )
    rows = P(DP_AXES, CTX_AXES, None)
    in_specs = (rows, rows, rows, rows, P(), P(), P(), P(), P(), rows)
    out_specs = (rows, rows, rows, rows, rows, P(DP_AXES, CTX_AXES), P(), P(), P(), P())
    return jax.shard_map(local, mesh=split, in_specs=in_specs, out_specs=out_specs, check_vma=False)
```

```python
import jax
import jax.numpy as jnp
from jax import lax
from jax.experimental import pallas as pl
from jax.experimental.pallas import tpu as pltpu
from jax.sharding import Mesh, PartitionSpec as P

D = 1920
HEADS = 8
HDIM = 128
SHORT = 7
LONG = 128
FCH = 128
FILTERS = 15
AD = HEADS * HDIM
FAR = 16
SMALL = 3 * SHORT + 3
CHUNK = 16
SPAN = 4 * LONG

DP_AXES = ("zl", "y")
CTX_AXES = ("xa", "xb", "zh", "c")
HEAD_AXES = ("xa", "zh")


def from_behind(x, by):
    peers = lax.axis_size(CTX_AXES)
    pairs = [(i, i + by) for i in range(peers) if 0 <= i + by < peers]
    return lax.ppermute(x, CTX_AXES, pairs)


def swap(x, axis):
    return lax.ppermute(x, axis, [(0, 1), (1, 0)])


def exchange(x, axes):
    return lax.all_to_all(x, axes, split_axis=0, concat_axis=0, tiled=True)


def toeplitz_kernel(forward_rows, backward_rows, forward_matrix, backward_matrix):
    for g in range(FILTERS):
        for rows, matrix in ((forward_rows, forward_matrix), (backward_rows, backward_matrix)):
            spread = jnp.broadcast_to(rows[g : g + 1, :], (LONG, 2 * LONG))
            matrix[g] = pltpu.roll(spread, 0, 1, stride=1, stride_axis=0).astype(jnp.bfloat16)


def toeplitz(filters):
    taps = filters.astype(jnp.float32)
    gap = jnp.zeros((FILTERS, LONG), jnp.float32)
    forward_rows = jnp.concatenate([gap[:, :1], taps[:, ::-1], gap[:, 1:]], axis=1)
    backward_rows = jnp.concatenate([taps, gap], axis=1)
    shape = jax.ShapeDtypeStruct((FILTERS, LONG, 2 * LONG), jnp.bfloat16)
    return pl.pallas_call(
        toeplitz_kernel,
        out_shape=[shape, shape],
        compiler_params=pltpu.CompilerParams(vmem_limit_bytes=16 * 1024 * 1024),
        cost_estimate=pl.CostEstimate(flops=4000000, bytes_accessed=2000000, transcendentals=0),
    )(forward_rows, backward_rows)


def turn_matrix(kind):
    first = lax.broadcasted_iota(jnp.int32, (LONG, LONG), 0)
    second = lax.broadcasted_iota(jnp.int32, (LONG, LONG), 1)
    return (first + second == LONG - 1).astype(kind)


def hyena_kernel(
    own,
    sides,
    x_all,
    cot_all,
    cot_next,
    cot_far,
    inv_rms,
    taps,
    gain,
    skip,
    forward_matrix,
    backward_matrix,
    layer_out,
    grad_residual,
    small,
    ext,
    cot_ext,
    prod,
    mix,
    stream,
    mixed,
    grad_prod,
    grad_stream,
    scaled_all,
    row_sum,
    reversed_sums,
):
    group = pl.program_id(0)
    groups = pl.num_programs(0)
    f32 = jnp.float32
    low = jnp.bfloat16
    edge = LONG + FAR
    columns = pl.ds(pl.multiple_of(group * FCH, FCH), FCH)

    @pl.when(group == 0)
    def _():
        prod[LONG + edge :, :] = jnp.zeros((LONG - FAR, FCH), low)
        mix[2 * LONG + FAR :, :] = jnp.zeros((LONG - FAR, FCH), low)
        row_sum[...] = jnp.zeros_like(row_sum)
        reversed_sums[...] = jnp.zeros_like(reversed_sums)
        small[groups] = jnp.zeros((SMALL, FCH), f32)

    ext[0:edge, :] = sides[0:edge, :].astype(f32)
    ext[edge : edge + LONG, :] = own[...].astype(f32)
    ext[edge + LONG :, :] = sides[edge:, :].astype(f32)
    cot_ext[0:LONG, :] = cot_all[:, columns].astype(f32)
    cot_ext[LONG : 2 * LONG, :] = cot_next[...].astype(f32)
    cot_ext[2 * LONG :, :] = cot_far[...].astype(f32)

    for first in range(-LONG, 2 * LONG + FAR, CHUNK):
        kinds = []
        if first >= 0:
            kinds.append(0)
        if first < edge:
            kinds += [1, 2]
        sums = {}
        for tap in range(SHORT):
            rows = ext[edge + first - tap : edge + first - tap + CHUNK, :]
            for kind in kinds:
                term = taps[kind * SHORT + tap : kind * SHORT + tap + 1, :] * rows
                sums[kind] = term if tap == 0 else sums[kind] + term
        if 1 in sums:
            prod[LONG + first : LONG + first + CHUNK, :] = (sums[1] * sums[2]).astype(low)
        if 0 in sums:
            mix[first : first + CHUNK, :] = (cot_ext[first : first + CHUNK, :] * sums[0]).astype(
                low
            )
        if 0 <= first < edge:
            for kind in range(3):
                stream[kind, first : first + CHUNK, :] = sums[kind]

    def product_of(matrix, rows):
        return jnp.dot(matrix, rows, preferred_element_type=f32)

    mixed[0:LONG, :] = product_of(forward_matrix[0], prod[0 : 2 * LONG, :])
    mixed[LONG:, :] = product_of(forward_matrix[0, 0:FAR, :], prod[LONG:, :])
    grad_prod[0:LONG, :] = product_of(backward_matrix[0], mix[0 : 2 * LONG, :])
    grad_prod[LONG:, :] = product_of(backward_matrix[0, 0:FAR, :], mix[LONG:, :])
    turned = product_of(turn_matrix(low), mix[0:LONG, :]).astype(low)
    table = lax.dot_general(
        turned, prod[0 : 2 * LONG, :], (((1,), (1,)), ((), ())), preferred_element_type=f32
    )
    table = pltpu.roll(table, 0, 1, stride=1, stride_axis=0)
    diagonals = jnp.sum(table[:, LONG:], axis=0, keepdims=True)
    reversed_sums[pl.ds(group, 1), :] = diagonals

    skip_row = skip[...]
    skip_sum = jnp.zeros((8, FCH), f32)
    for first in range(0, edge, CHUNK):
        rows = slice(first, first + CHUNK)
        prod_rows = prod[LONG + first : LONG + first + CHUNK, :].astype(f32)
        mix_rows = mix[rows, :].astype(f32)
        mixed_rows = mixed[rows, :] + skip_row * prod_rows
        grad_rows = grad_prod[rows, :] + skip_row * mix_rows
        grad_stream[0, rows, :] = cot_ext[rows, :] * mixed_rows
        grad_stream[1, rows, :] = grad_rows * stream[2, rows, :]
        grad_stream[2, rows, :] = grad_rows * stream[1, rows, :]
        if first < LONG:
            x_rows = x_all[rows, columns].astype(f32)
            layer_out[rows, :] = (x_rows + stream[0, rows, :] * mixed_rows).astype(low)
            skip_sum = skip_sum + jnp.sum((mix_rows * prod_rows).reshape(-1, 8, FCH), axis=0)

    gain_row = gain[...]
    gain_sum = jnp.zeros((8, FCH), f32)
    tap_sums = [None] * (3 * SHORT)
    for first in range(0, LONG, CHUNK):
        rows = slice(first, first + CHUNK)
        grad_normed = None
        for tap in range(SHORT):
            normed_rows = ext[edge + first - tap : edge + first - tap + CHUNK, :]
            for kind in range(3):
                at = kind * SHORT + tap
                term = taps[at : at + 1, :] * grad_stream[kind, first + tap : first + tap + CHUNK, :]
                grad_normed = term if grad_normed is None else grad_normed + term
                part = jnp.sum(
                    (grad_stream[kind, rows, :] * normed_rows).reshape(-1, 8, FCH), axis=0
                )
                tap_sums[at] = part if first == 0 else tap_sums[at] + part
        x_rows = x_all[rows, columns].astype(f32)
        scaled = grad_normed * gain_row
        scaled_all[group, rows, :] = scaled
        row_sum[rows, :] = row_sum[rows, :] + scaled * x_rows
        gain_sum = gain_sum + jnp.sum(
            (grad_normed * x_rows * inv_rms[rows, :]).reshape(-1, 8, FCH), axis=0
        )
    for at in range(3 * SHORT):
        small[group, at : at + 1, :] = jnp.sum(tap_sums[at], axis=0, keepdims=True)
    small[group, 3 * SHORT : 3 * SHORT + 1, :] = jnp.sum(gain_sum, axis=0, keepdims=True)
    small[group, 3 * SHORT + 1 : 3 * SHORT + 2, :] = jnp.sum(skip_sum, axis=0, keepdims=True)

    @pl.when(group == groups - 1)
    def _():
        filter_sums = jnp.dot(
            reversed_sums[...], turn_matrix(f32), precision=lax.Precision.HIGHEST, preferred_element_type=f32
        )
        for g in range(FILTERS):
            small[g, SMALL - 1 : SMALL, :] = filter_sums[g : g + 1, :]
        scale = inv_rms[...]
        mean = jnp.sum(row_sum[...], axis=1, keepdims=True) * (1.0 / D)
        factor = scale * scale * mean
        for g in range(FILTERS):
            cols = slice(g * FCH, (g + 1) * FCH)
            x_cols = x_all[:, cols].astype(f32)
            grad = cot_all[:, cols].astype(f32) + scale * (scaled_all[g] - x_cols * factor)
            grad_residual[:, cols] = grad.astype(low)


def hyena(normed, sides, x_first, cotangent, cot_sides, inv_rms, taps, gain, skip, matrices):
    rows = x_first.shape[0]
    f32 = jnp.float32

    def part(count):
        return pl.BlockSpec((count, FCH), lambda g: (0, g))

    def whole(shape):
        return pl.BlockSpec(shape, lambda g: (0,) * len(shape))

    per_group = pl.BlockSpec((1, LONG, 2 * LONG), lambda g: (g, 0, 0))
    edge = LONG + FAR
    return pl.pallas_call(
        hyena_kernel,
        grid=(FILTERS,),
        in_specs=[
            part(rows),
            part(2 * edge),
            whole((rows, D)),
            whole((rows, D)),
            part(rows),
            part(FAR),
            whole((rows, 1)),
            part(3 * SHORT),
            part(1),
            part(1),
            per_group,
            per_group,
        ],
        out_specs=[
            part(rows),
            whole((rows, D)),
            whole((FILTERS + 1, SMALL, FCH)),
        ],
        out_shape=[
            jax.ShapeDtypeStruct((rows, D), jnp.bfloat16),
            jax.ShapeDtypeStruct((rows, D), jnp.bfloat16),
            jax.ShapeDtypeStruct((FILTERS + 1, SMALL, FCH), f32),
        ],
        scratch_shapes=[
            pltpu.VMEM((3 * LONG + 2 * FAR, FCH), f32),
            pltpu.VMEM((2 * LONG + FAR, FCH), f32),
            pltpu.VMEM((3 * LONG, FCH), jnp.bfloat16),
            pltpu.VMEM((3 * LONG, FCH), jnp.bfloat16),
            pltpu.VMEM((3, edge, FCH), f32),
            pltpu.VMEM((edge, FCH), f32),
            pltpu.VMEM((edge, FCH), f32),
            pltpu.VMEM((3, edge, FCH), f32),
            pltpu.VMEM((FILTERS, LONG, FCH), f32),
            pltpu.VMEM((LONG, FCH), f32),
            pltpu.VMEM((FILTERS + 1, FCH), f32),
        ],
        compiler_params=pltpu.CompilerParams(
            dimension_semantics=("arbitrary",), vmem_limit_bytes=32 * 1024 * 1024
        ),
        cost_estimate=pl.CostEstimate(
            flops=2 * 4 * 1024 * 1024 * 60, bytes_accessed=12 * 1024 * 1024, transcendentals=0
        ),
    )(
        normed,
        sides,
        x_first,
        cotangent,
        cot_sides[0],
        cot_sides[1],
        inv_rms,
        taps.reshape(3 * SHORT, D),
        gain.reshape(1, D),
        skip.reshape(1, D),
        matrices[0],
        matrices[1],
    )


def allowed_keys(kind, core):
    keys = lax.broadcasted_iota(jnp.int32, (SPAN, SPAN), 0)
    queries = lax.broadcasted_iota(jnp.int32, (SPAN, SPAN), 1)
    if kind == 0:
        return queries >= keys
    return queries // LONG + core > keys // LONG


def spans_of(half):
    base = 4 * half
    spans = [(base, 0), (base + 2, 1), (base + 1, 2), (base + 3, 2)]
    return spans + [(span, 3) for span in range(base)]


def logits_of(k_rows, q_rows, kind, core):
    logits = lax.dot_general(
        k_rows, q_rows, (((1,), (1,)), ((), ())), preferred_element_type=jnp.float32
    ) * (HDIM**-0.5)
    if kind < 2:
        logits = jnp.where(allowed_keys(kind, core), logits, -jnp.inf)
    return logits


def key_rows(parts, span):
    ref = parts[span // 2 % 2][span % 2]
    first = span // 4 * 4
    keys = ref[first : first + 4, 0:LONG, :].reshape(SPAN, HDIM)
    values = ref[first : first + 4, LONG:, :].reshape(SPAN, HDIM)
    return keys, values


def attend_kernel(
    place, query, own, far, own_c, far_c, out, log_total, top, total, wide
):
    parts = ((own, far), (own_c, far_c))
    f32 = jnp.float32
    for half in range(2):
        q_rows = query[half * SPAN : (half + 1) * SPAN, :]
        for span, kind in spans_of(half):

            def visit(span=span, kind=kind):
                k_rows, v_rows = key_rows(parts, span)
                logits = logits_of(k_rows, q_rows, kind, place[1])
                high = jnp.max(logits, axis=0, keepdims=True)
                if kind > 0:
                    high = jnp.maximum(high, top[...])
                probs = jnp.exp(logits - high)
                part = jnp.sum(probs, axis=0, keepdims=True)
                values = lax.dot_general(
                    v_rows,
                    probs.astype(jnp.bfloat16),
                    (((0,), (0,)), ((), ())),
                    preferred_element_type=f32,
                )
                if kind > 0:
                    shrink = jnp.exp(top[...] - high)
                    part = part + total[...] * shrink
                    values = values + wide[...] * shrink
                top[...] = high
                total[...] = part
                wide[...] = values

            if kind == 2:
                pl.when(place[0] == 1)(visit)
            else:
                visit()
        columns = slice(half * SPAN, (half + 1) * SPAN)
        out[columns, :] = (wide[...] / total[...]).T.astype(jnp.bfloat16)
        log_total[:, columns] = top[...] + jnp.log(total[...])


def attend(place, query, kv):
    count = query.shape[0]
    return pl.pallas_call(
        attend_kernel,
        in_specs=[pl.BlockSpec(memory_space=pltpu.SMEM)]
        + [pl.BlockSpec(memory_space=pltpu.VMEM)] * 5,
        out_shape=[
            jax.ShapeDtypeStruct((count, HDIM), jnp.bfloat16),
            jax.ShapeDtypeStruct((1, count), jnp.float32),
        ],
        scratch_shapes=[
            pltpu.VMEM((1, SPAN), jnp.float32),
            pltpu.VMEM((1, SPAN), jnp.float32),
            pltpu.VMEM((HDIM, SPAN), jnp.float32),
        ],
        compiler_params=pltpu.CompilerParams(vmem_limit_bytes=32 * 1024 * 1024),
        cost_estimate=pl.CostEstimate(
            flops=1600000000, bytes_accessed=3000000, transcendentals=3000000
        ),
    )(place, query, *kv)


def attend_back_kernel(
    place,
    query,
    own,
    far,
    own_c,
    far_c,
    out,
    log_total,
    grad_out,
    grad_query,
    same_core,
    other_core,
    sums,
    wide,
):
    parts = ((own, far), (own_c, far_c))
    f32 = jnp.float32
    low = jnp.bfloat16
    scale = HDIM**-0.5
    for half in range(2):
        columns = slice(half * SPAN, (half + 1) * SPAN)
        q_rows = query[columns, :]
        g_rows = grad_out[columns, :]
        both = g_rows.astype(f32) * out[columns, :].astype(f32)
        delta = jnp.sum(both.T, axis=0, keepdims=True)
        log_row = log_total[:, columns]
        for span, kind in spans_of(half):
            rows = slice(span * SPAN, (span + 1) * SPAN)
            fresh = half == 1 and span >= 4 or half == 0

            def visit(rows=rows, span=span, kind=kind, fresh=fresh):
                k_rows, v_rows = key_rows(parts, span)
                logits = logits_of(k_rows, q_rows, kind, place[1])
                probs = jnp.exp(logits - log_row)
                grad_probs = lax.dot_general(
                    v_rows,
                    g_rows,
                    (((1,), (1,)), ((), ())),
                    preferred_element_type=f32,
                )
                grad_logits = (probs * (grad_probs - delta)).astype(low)
                grad_k = jnp.dot(grad_logits, q_rows, preferred_element_type=f32)
                grad_v = jnp.dot(probs.astype(low), g_rows, preferred_element_type=f32)
                if fresh:
                    sums[rows, 0:HDIM] = grad_k
                    sums[rows, HDIM:] = grad_v
                else:
                    sums[rows, 0:HDIM] += grad_k
                    sums[rows, HDIM:] += grad_v
                part = lax.dot_general(
                    k_rows, grad_logits, (((0,), (0,)), ((), ())), preferred_element_type=f32
                )
                wide[...] = part if kind == 0 else wide[...] + part

            if kind == 2:
                pl.when(place[0] == 1)(visit)

                @pl.when(place[0] == 0)
                def _(rows=rows):
                    sums[rows, :] = jnp.zeros((SPAN, 2 * HDIM), f32)
            else:
                visit()
        grad_query[columns, :] = (wide[...] * scale).T.astype(low)
    for xa in range(2):
        for cr, target in ((0, same_core), (1, other_core)):
            for xr in range(2):
                span = xa * 4 + cr * 2 + xr
                rows = slice(span * SPAN, (span + 1) * SPAN)
                target[xa, xr, :, 0:HDIM] = (sums[rows, 0:HDIM] * scale).astype(low)
                target[xa, xr, :, HDIM:] = sums[rows, HDIM:].astype(low)


def attend_back(place, query, kv, out, log_total, grad_out):
    vmem = pl.BlockSpec(memory_space=pltpu.VMEM)
    part = jax.ShapeDtypeStruct((2, 2, SPAN, 2 * HDIM), jnp.bfloat16)
    return pl.pallas_call(
        attend_back_kernel,
        in_specs=[pl.BlockSpec(memory_space=pltpu.SMEM)] + [vmem] * 8,
        out_shape=[jax.ShapeDtypeStruct(query.shape, jnp.bfloat16), part, part],
        scratch_shapes=[
            pltpu.VMEM((8 * SPAN, 2 * HDIM), jnp.float32),
            pltpu.VMEM((HDIM, SPAN), jnp.float32),
        ],
        compiler_params=pltpu.CompilerParams(vmem_limit_bytes=40 * 1024 * 1024),
        cost_estimate=pl.CostEstimate(
            flops=4000000000, bytes_accessed=6000000, transcendentals=3000000
        ),
    )(place, query, *kv, out, log_total, grad_out)


def both_sides(rows):
    return (
        from_behind(rows[-FAR:], 2),
        from_behind(rows, 1),
        from_behind(rows, -1),
        from_behind(rows[:FAR], -2),
    )


def first_norm(residual, attention, w_out, norm_gain):
    x_float = residual.astype(jnp.float32) + jnp.dot(
        attention, w_out, preferred_element_type=jnp.float32
    )
    x_first = lax.optimization_barrier(x_float.astype(jnp.bfloat16))
    x_float = x_first.astype(jnp.float32)
    inv_rms = lax.rsqrt(jnp.mean(x_float * x_float, axis=-1, keepdims=True) + 1e-05)
    normed = lax.optimization_barrier((x_float * inv_rms * norm_gain).astype(jnp.bfloat16))
    return x_first, inv_rms, normed


def to_heads(rows_in):
    return rows_in.reshape(rows_in.shape[0], HEADS, HDIM).transpose(1, 0, 2)


def from_heads(pieces):
    return pieces.transpose(1, 0, 2).reshape(pieces.shape[1], HEADS * HDIM)


def gather_keys(own):
    far = swap(own, "xb")
    return own, far, swap(own, "c"), swap(far, "c")


def weight_pieces(attention, grad_residual):
    core = lax.axis_index("c")
    half = AD // 2
    mine = jnp.where(core == 0, attention[:, :half], attention[:, half:])
    theirs = jnp.where(core == 0, attention[:, half:], attention[:, :half])
    rows_a = jnp.concatenate([mine, swap(theirs, "c")], axis=0)
    rows_g = jnp.concatenate([grad_residual, swap(grad_residual, "c")], axis=0)
    peers = lax.axis_size("y")
    width = half // peers
    at = lax.axis_index("y")
    pieces = []
    for step in range(peers):
        columns = lax.dynamic_slice_in_dim(rows_a, (at + step) % peers * width, width, axis=1)
        piece = lax.dot_general(
            rows_g, columns, (((0,), (0,)), ((), ())), preferred_element_type=jnp.float32
        )
        pieces.append(piece.astype(jnp.bfloat16))
    return lax.optimization_barrier(pieces)


def weight_over_y(pieces):
    peers = len(pieces)
    total = pieces[0].astype(jnp.float32)
    for step in range(1, peers):
        pairs = [(i, (i + step) % peers) for i in range(peers)]
        total = total + lax.ppermute(pieces[step], "y", pairs).astype(jnp.float32)
    return total.astype(jnp.bfloat16)


def weight_over_zl(total):
    zl = lax.axis_index("zl")
    total = total.reshape(16, 2, D // 32, -1)
    halves = (total[:, 0], total[:, 1])
    received = []
    for turn in range(2):
        piece = jnp.where(zl == 0, halves[turn], halves[1 - turn])
        pairs = [(a * 2 + b, b * 2 + (a ^ turn)) for a in range(2) for b in range(2)]
        received.append(lax.ppermute(piece, ("zl", "c"), pairs).astype(jnp.float32))
    return (received[0] + received[1]).astype(jnp.bfloat16)


def weight_over_xb(total):
    xb = lax.axis_index("xb")
    total = total.reshape(2, 2, 4, D // 32, -1)
    mine = jnp.where(xb == 0, total[:, 0], total[:, 1]).astype(jnp.float32)
    theirs = jnp.where(xb == 0, total[:, 1], total[:, 0])
    total = mine + swap(theirs, "xb").astype(jnp.float32)
    return total.astype(jnp.bfloat16).reshape(8, D // 32, -1)


def local(
    query_in,
    key_in,
    value_in,
    residual,
    w_out,
    norm_gain,
    short_taps,
    filters,
    skip_gain,
    cotangent,
):
    tok_rows = query_in.shape[1]
    matrices = toeplitz(filters)
    qkv_send = jnp.concatenate(
        [to_heads(query_in[0]), to_heads(key_in[0]), to_heads(value_in[0])], axis=1
    )
    qkv_own = exchange(qkv_send, HEAD_AXES)
    query_rows = qkv_own[:, :tok_rows].reshape(8 * tok_rows, HDIM)
    kv_all = gather_keys(qkv_own[:, tok_rows:])
    apart = lax.optimization_barrier((residual[0], cotangent[0], qkv_own))
    res_sides = both_sides(apart[0])
    cot_sides = (from_behind(apart[1], -1), from_behind(apart[1][:FAR], -2))
    query_total = 8 * tok_rows
    place = jnp.stack([lax.axis_index("xb"), lax.axis_index("c")]).astype(jnp.int32)
    head_out, log_total = attend(place, query_rows, kv_all)
    head_out, res_sides, cot_sides = lax.optimization_barrier((head_out, res_sides, cot_sides))
    attention = from_heads(exchange(head_out.reshape(8, tok_rows, HDIM), HEAD_AXES))
    att_sides = both_sides(attention)
    x_first, inv_rms, normed = first_norm(residual[0], attention, w_out, norm_gain)
    _, _, sides = first_norm(
        jnp.concatenate(res_sides), jnp.concatenate(att_sides), w_out, norm_gain
    )
    layer_out, grad_residual, small = hyena(
        normed,
        sides,
        x_first,
        cotangent[0],
        cot_sides,
        inv_rms,
        short_taps,
        norm_gain,
        skip_gain,
        matrices,
    )

    grad_attention = jnp.einsum(
        "td,ad->ta", grad_residual, w_out, preferred_element_type=jnp.float32
    ).astype(jnp.bfloat16)
    small_rows = (FILTERS + 1) * SMALL // 8
    small_send = small.reshape(8, small_rows, HDIM).astype(jnp.bfloat16)
    grad_recv = exchange(
        jnp.concatenate([to_heads(grad_attention), small_send], axis=1), HEAD_AXES
    )
    weight_part = weight_over_y(weight_pieces(attention, grad_residual))
    grad_rows_all = grad_recv[:, :tok_rows].reshape(query_total, HDIM)
    small_part = jnp.sum(grad_recv[:, tok_rows:].astype(jnp.float32), axis=0)
    grad_query, same_core, other_core = attend_back(
        place, query_rows, kv_all, head_out, log_total, grad_rows_all
    )
    dq_send = grad_query.reshape(8, tok_rows, HDIM)
    dkv = same_core.astype(jnp.float32) + swap(other_core, "c").astype(jnp.float32)
    dkv_far = swap(dkv[:, 1].astype(jnp.bfloat16), "xb")
    small_part, _ = lax.optimization_barrier((small_part, grad_query))
    sequences = lax.axis_size(DP_AXES)
    small_part = exchange(
        jnp.broadcast_to(small_part[None], (sequences,) + small_part.shape), DP_AXES
    )
    small_part = jnp.sum(small_part, axis=0)
    small_part = small_part + swap(small_part, "c")
    small_part = small_part + swap(small_part, "xb")
    small_part = small_part.astype(jnp.bfloat16)
    weight_part = weight_over_zl(weight_part)
    weight_part, _ = lax.optimization_barrier((weight_part, dkv_far))
    dkv = dkv[:, 0] + dkv_far.astype(jnp.float32)
    dkv = dkv.reshape(8, tok_rows, 2 * HDIM).astype(jnp.bfloat16)
    weight_part = weight_over_xb(weight_part)
    weight_rows = weight_part.size // (8 * HDIM)
    last_send = jnp.concatenate(
        [
            dq_send,
            dkv[:, :, :HDIM],
            dkv[:, :, HDIM:],
            jnp.broadcast_to(small_part[None], (8,) + small_part.shape),
            weight_part.reshape(8, weight_rows, HDIM),
        ],
        axis=1,
    )
    last = exchange(last_send, HEAD_AXES)
    grad_query = from_heads(last[:, :tok_rows])
    grad_key = from_heads(last[:, tok_rows : 2 * tok_rows])
    grad_value = from_heads(last[:, 2 * tok_rows : 3 * tok_rows])
    sums_back = last[:, 3 * tok_rows :].astype(jnp.float32)
    small_back = sums_back[:, :small_rows]
    small_back = small_back.reshape(FILTERS + 1, SMALL, FCH)[:FILTERS].transpose(1, 0, 2)
    grad_filters = small_back[SMALL - 1]
    small_back = small_back.reshape(SMALL, D)
    grad_weight = jnp.sum(sums_back[:, small_rows:], axis=0)
    grad_weight = grad_weight.reshape(D // 32, -1).T
    return (
        layer_out[None],
        grad_residual[None],
        grad_query[None],
        grad_key[None],
        grad_value[None],
        grad_weight,
        small_back[3 * SHORT],
        small_back[: 3 * SHORT].reshape(3, SHORT, D),
        grad_filters,
        small_back[3 * SHORT + 1],
    )


def solution(mesh):
    sequences = mesh.shape["dp"]
    split = Mesh(
        mesh.devices.reshape(2, sequences // 2, 2, 2, 4, 2), DP_AXES + CTX_AXES
    )
    rows = P(DP_AXES, CTX_AXES, None)
    in_specs = (rows, rows, rows, rows, P(), P(), P(), P(), P(), rows)
    out_specs = (rows, rows, rows, rows, rows, P(DP_AXES, CTX_AXES), P(), P(), P(), P())
    return jax.shard_map(local, mesh=split, in_specs=in_specs, out_specs=out_specs, check_vma=False)
```

```python
import jax
import jax.numpy as jnp
from jax import lax
from jax.experimental import pallas as pl
from jax.experimental.pallas import tpu as pltpu
from jax.sharding import Mesh, PartitionSpec as P

D = 1920
HEADS = 8
HDIM = 128
SHORT = 7
LONG = 128
FCH = 128
FILTERS = 15
AD = HEADS * HDIM
FAR = 16
SMALL = 3 * SHORT + 3
CHUNK = 16
SPAN = 4 * LONG

DP_AXES = ("zl", "y")
CTX_AXES = ("xa", "xb", "zh", "c")
HEAD_AXES = ("xa", "zh")


def from_behind(x, by):
    peers = lax.axis_size(CTX_AXES)
    pairs = [(i, i + by) for i in range(peers) if 0 <= i + by < peers]
    return lax.ppermute(x, CTX_AXES, pairs)


def swap(x, axis):
    return lax.ppermute(x, axis, [(0, 1), (1, 0)])


def exchange(x, axes):
    return lax.all_to_all(x, axes, split_axis=0, concat_axis=0, tiled=True)


def toeplitz_kernel(forward_rows, backward_rows, forward_matrix, backward_matrix):
    for g in range(FILTERS):
        for rows, matrix in ((forward_rows, forward_matrix), (backward_rows, backward_matrix)):
            spread = jnp.broadcast_to(rows[g : g + 1, :], (LONG, 2 * LONG))
            matrix[g] = pltpu.roll(spread, 0, 1, stride=1, stride_axis=0).astype(jnp.bfloat16)


def toeplitz(filters):
    taps = filters.astype(jnp.float32)
    gap = jnp.zeros((FILTERS, LONG), jnp.float32)
    forward_rows = jnp.concatenate([gap[:, :1], taps[:, ::-1], gap[:, 1:]], axis=1)
    backward_rows = jnp.concatenate([taps, gap], axis=1)
    shape = jax.ShapeDtypeStruct((FILTERS, LONG, 2 * LONG), jnp.bfloat16)
    return pl.pallas_call(
        toeplitz_kernel,
        out_shape=[shape, shape],
        compiler_params=pltpu.CompilerParams(vmem_limit_bytes=16 * 1024 * 1024),
        cost_estimate=pl.CostEstimate(flops=4000000, bytes_accessed=2000000, transcendentals=0),
    )(forward_rows, backward_rows)


def turn_matrix(kind):
    first = lax.broadcasted_iota(jnp.int32, (LONG, LONG), 0)
    second = lax.broadcasted_iota(jnp.int32, (LONG, LONG), 1)
    return (first + second == LONG - 1).astype(kind)


def hyena_kernel(
    own,
    sides,
    x_all,
    cot_all,
    cot_next,
    cot_far,
    inv_rms,
    taps,
    gain,
    skip,
    forward_matrix,
    backward_matrix,
    layer_out,
    grad_residual,
    small,
    ext,
    cot_ext,
    prod,
    mix,
    stream,
    mixed,
    grad_prod,
    grad_stream,
    scaled_all,
    row_sum,
    reversed_sums,
):
    group = pl.program_id(0)
    groups = pl.num_programs(0)
    f32 = jnp.float32
    low = jnp.bfloat16
    edge = LONG + FAR
    columns = pl.ds(pl.multiple_of(group * FCH, FCH), FCH)

    @pl.when(group == 0)
    def _():
        prod[LONG + edge :, :] = jnp.zeros((LONG - FAR, FCH), low)
        mix[2 * LONG + FAR :, :] = jnp.zeros((LONG - FAR, FCH), low)
        row_sum[...] = jnp.zeros_like(row_sum)
        reversed_sums[...] = jnp.zeros_like(reversed_sums)
        small[groups] = jnp.zeros((SMALL, FCH), f32)

    ext[0:edge, :] = sides[0:edge, :].astype(f32)
    ext[edge : edge + LONG, :] = own[...].astype(f32)
    ext[edge + LONG :, :] = sides[edge:, :].astype(f32)
    cot_ext[0:LONG, :] = cot_all[:, columns].astype(f32)
    cot_ext[LONG : 2 * LONG, :] = cot_next[...].astype(f32)
    cot_ext[2 * LONG :, :] = cot_far[...].astype(f32)

    for first in range(-LONG, 2 * LONG + FAR, CHUNK):
        kinds = []
        if first >= 0:
            kinds.append(0)
        if first < edge:
            kinds += [1, 2]
        sums = {}
        for tap in range(SHORT):
            rows = ext[edge + first - tap : edge + first - tap + CHUNK, :]
            for kind in kinds:
                term = taps[kind * SHORT + tap : kind * SHORT + tap + 1, :] * rows
                sums[kind] = term if tap == 0 else sums[kind] + term
        if 1 in sums:
            prod[LONG + first : LONG + first + CHUNK, :] = (sums[1] * sums[2]).astype(low)
        if 0 in sums:
            mix[first : first + CHUNK, :] = (cot_ext[first : first + CHUNK, :] * sums[0]).astype(
                low
            )
        if 0 <= first < edge:
            for kind in range(3):
                stream[kind, first : first + CHUNK, :] = sums[kind]

    def product_of(matrix, rows):
        return jnp.dot(matrix, rows, preferred_element_type=f32)

    mixed[0:LONG, :] = product_of(forward_matrix[0], prod[0 : 2 * LONG, :])
    mixed[LONG:, :] = product_of(forward_matrix[0, 0:FAR, :], prod[LONG:, :])
    grad_prod[0:LONG, :] = product_of(backward_matrix[0], mix[0 : 2 * LONG, :])
    grad_prod[LONG:, :] = product_of(backward_matrix[0, 0:FAR, :], mix[LONG:, :])
    turned = product_of(turn_matrix(low), mix[0:LONG, :]).astype(low)
    table = lax.dot_general(
        turned, prod[0 : 2 * LONG, :], (((1,), (1,)), ((), ())), preferred_element_type=f32
    )
    table = pltpu.roll(table, 0, 1, stride=1, stride_axis=0)
    diagonals = jnp.sum(table[:, LONG:], axis=0, keepdims=True)
    reversed_sums[pl.ds(group, 1), :] = diagonals

    skip_row = skip[...]
    skip_sum = jnp.zeros((8, FCH), f32)
    for first in range(0, edge, CHUNK):
        rows = slice(first, first + CHUNK)
        prod_rows = prod[LONG + first : LONG + first + CHUNK, :].astype(f32)
        mix_rows = mix[rows, :].astype(f32)
        mixed_rows = mixed[rows, :] + skip_row * prod_rows
        grad_rows = grad_prod[rows, :] + skip_row * mix_rows
        grad_stream[0, rows, :] = cot_ext[rows, :] * mixed_rows
        grad_stream[1, rows, :] = grad_rows * stream[2, rows, :]
        grad_stream[2, rows, :] = grad_rows * stream[1, rows, :]
        if first < LONG:
            x_rows = x_all[rows, columns].astype(f32)
            layer_out[rows, :] = (x_rows + stream[0, rows, :] * mixed_rows).astype(low)
            skip_sum = skip_sum + jnp.sum((mix_rows * prod_rows).reshape(-1, 8, FCH), axis=0)

    gain_row = gain[...]
    gain_sum = jnp.zeros((8, FCH), f32)
    tap_sums = [None] * (3 * SHORT)
    for first in range(0, LONG, CHUNK):
        rows = slice(first, first + CHUNK)
        grad_normed = None
        for tap in range(SHORT):
            normed_rows = ext[edge + first - tap : edge + first - tap + CHUNK, :]
            for kind in range(3):
                at = kind * SHORT + tap
                term = taps[at : at + 1, :] * grad_stream[kind, first + tap : first + tap + CHUNK, :]
                grad_normed = term if grad_normed is None else grad_normed + term
                part = jnp.sum(
                    (grad_stream[kind, rows, :] * normed_rows).reshape(-1, 8, FCH), axis=0
                )
                tap_sums[at] = part if first == 0 else tap_sums[at] + part
        x_rows = x_all[rows, columns].astype(f32)
        scaled = grad_normed * gain_row
        scaled_all[group, rows, :] = scaled
        row_sum[rows, :] = row_sum[rows, :] + scaled * x_rows
        gain_sum = gain_sum + jnp.sum(
            (grad_normed * x_rows * inv_rms[rows, :]).reshape(-1, 8, FCH), axis=0
        )
    for at in range(3 * SHORT):
        small[group, at : at + 1, :] = jnp.sum(tap_sums[at], axis=0, keepdims=True)
    small[group, 3 * SHORT : 3 * SHORT + 1, :] = jnp.sum(gain_sum, axis=0, keepdims=True)
    small[group, 3 * SHORT + 1 : 3 * SHORT + 2, :] = jnp.sum(skip_sum, axis=0, keepdims=True)

    @pl.when(group == groups - 1)
    def _():
        filter_sums = jnp.dot(
            reversed_sums[...], turn_matrix(f32), precision=lax.Precision.HIGHEST, preferred_element_type=f32
        )
        for g in range(FILTERS):
            small[g, SMALL - 1 : SMALL, :] = filter_sums[g : g + 1, :]
        scale = inv_rms[...]
        mean = jnp.sum(row_sum[...], axis=1, keepdims=True) * (1.0 / D)
        factor = scale * scale * mean
        for g in range(FILTERS):
            cols = slice(g * FCH, (g + 1) * FCH)
            x_cols = x_all[:, cols].astype(f32)
            grad = cot_all[:, cols].astype(f32) + scale * (scaled_all[g] - x_cols * factor)
            grad_residual[:, cols] = grad.astype(low)


def hyena(normed, sides, x_first, cotangent, cot_sides, inv_rms, taps, gain, skip, matrices):
    rows = x_first.shape[0]
    f32 = jnp.float32

    def part(count):
        return pl.BlockSpec((count, FCH), lambda g: (0, g))

    def whole(shape):
        return pl.BlockSpec(shape, lambda g: (0,) * len(shape))

    per_group = pl.BlockSpec((1, LONG, 2 * LONG), lambda g: (g, 0, 0))
    edge = LONG + FAR
    return pl.pallas_call(
        hyena_kernel,
        grid=(FILTERS,),
        in_specs=[
            part(rows),
            part(2 * edge),
            whole((rows, D)),
            whole((rows, D)),
            part(rows),
            part(FAR),
            whole((rows, 1)),
            part(3 * SHORT),
            part(1),
            part(1),
            per_group,
            per_group,
        ],
        out_specs=[
            part(rows),
            whole((rows, D)),
            whole((FILTERS + 1, SMALL, FCH)),
        ],
        out_shape=[
            jax.ShapeDtypeStruct((rows, D), jnp.bfloat16),
            jax.ShapeDtypeStruct((rows, D), jnp.bfloat16),
            jax.ShapeDtypeStruct((FILTERS + 1, SMALL, FCH), f32),
        ],
        scratch_shapes=[
            pltpu.VMEM((3 * LONG + 2 * FAR, FCH), f32),
            pltpu.VMEM((2 * LONG + FAR, FCH), f32),
            pltpu.VMEM((3 * LONG, FCH), jnp.bfloat16),
            pltpu.VMEM((3 * LONG, FCH), jnp.bfloat16),
            pltpu.VMEM((3, edge, FCH), f32),
            pltpu.VMEM((edge, FCH), f32),
            pltpu.VMEM((edge, FCH), f32),
            pltpu.VMEM((3, edge, FCH), f32),
            pltpu.VMEM((FILTERS, LONG, FCH), f32),
            pltpu.VMEM((LONG, FCH), f32),
            pltpu.VMEM((FILTERS + 1, FCH), f32),
        ],
        compiler_params=pltpu.CompilerParams(
            dimension_semantics=("arbitrary",), vmem_limit_bytes=32 * 1024 * 1024
        ),
        cost_estimate=pl.CostEstimate(
            flops=2 * 4 * 1024 * 1024 * 60, bytes_accessed=12 * 1024 * 1024, transcendentals=0
        ),
    )(
        normed,
        sides,
        x_first,
        cotangent,
        cot_sides[0],
        cot_sides[1],
        inv_rms,
        taps.reshape(3 * SHORT, D),
        gain.reshape(1, D),
        skip.reshape(1, D),
        matrices[0],
        matrices[1],
    )


def allowed_keys(kind, core):
    keys = lax.broadcasted_iota(jnp.int32, (SPAN, SPAN), 0)
    queries = lax.broadcasted_iota(jnp.int32, (SPAN, SPAN), 1)
    if kind == 0:
        return queries >= keys
    return queries // LONG + core > keys // LONG


def spans_of(half):
    base = 4 * half
    spans = [(base, 0), (base + 2, 1), (base + 1, 2), (base + 3, 2)]
    return spans + [(span, 3) for span in range(base)]


def logits_of(k_rows, q_rows, kind, core):
    logits = lax.dot_general(
        k_rows, q_rows, (((1,), (1,)), ((), ())), preferred_element_type=jnp.float32
    ) * (HDIM**-0.5)
    if kind < 2:
        logits = jnp.where(allowed_keys(kind, core), logits, -jnp.inf)
    return logits


def key_rows(parts, span):
    ref = parts[span // 2 % 2][span % 2]
    first = span // 4 * 4
    keys = ref[first : first + 4, 0:LONG, :].reshape(SPAN, HDIM)
    values = ref[first : first + 4, LONG:, :].reshape(SPAN, HDIM)
    return keys, values


def attend_kernel(
    place, query, own, far, own_c, far_c, out, log_total, top, total, wide
):
    parts = ((own, far), (own_c, far_c))
    f32 = jnp.float32
    for half in range(2):
        q_rows = query[half * SPAN : (half + 1) * SPAN, :]
        for span, kind in spans_of(half):

            def visit(span=span, kind=kind):
                k_rows, v_rows = key_rows(parts, span)
                logits = logits_of(k_rows, q_rows, kind, place[1])
                high = jnp.max(logits, axis=0, keepdims=True)
                if kind > 0:
                    high = jnp.maximum(high, top[...])
                probs = jnp.exp(logits - high)
                part = jnp.sum(probs, axis=0, keepdims=True)
                values = lax.dot_general(
                    v_rows,
                    probs.astype(jnp.bfloat16),
                    (((0,), (0,)), ((), ())),
                    preferred_element_type=f32,
                )
                if kind > 0:
                    shrink = jnp.exp(top[...] - high)
                    part = part + total[...] * shrink
                    values = values + wide[...] * shrink
                top[...] = high
                total[...] = part
                wide[...] = values

            if kind == 2:
                pl.when(place[0] == 1)(visit)
            else:
                visit()
        columns = slice(half * SPAN, (half + 1) * SPAN)
        out[columns, :] = (wide[...] / total[...]).T.astype(jnp.bfloat16)
        log_total[:, columns] = top[...] + jnp.log(total[...])


def attend(place, query, kv):
    count = query.shape[0]
    return pl.pallas_call(
        attend_kernel,
        in_specs=[pl.BlockSpec(memory_space=pltpu.SMEM)]
        + [pl.BlockSpec(memory_space=pltpu.VMEM)] * 5,
        out_shape=[
            jax.ShapeDtypeStruct((count, HDIM), jnp.bfloat16),
            jax.ShapeDtypeStruct((1, count), jnp.float32),
        ],
        scratch_shapes=[
            pltpu.VMEM((1, SPAN), jnp.float32),
            pltpu.VMEM((1, SPAN), jnp.float32),
            pltpu.VMEM((HDIM, SPAN), jnp.float32),
        ],
        compiler_params=pltpu.CompilerParams(vmem_limit_bytes=32 * 1024 * 1024),
        cost_estimate=pl.CostEstimate(
            flops=1600000000, bytes_accessed=3000000, transcendentals=3000000
        ),
    )(place, query, *kv)


def attend_back_kernel(
    place,
    query,
    own,
    far,
    own_c,
    far_c,
    out,
    log_total,
    grad_out,
    grad_query,
    same_core,
    other_core,
    sums,
    wide,
):
    parts = ((own, far), (own_c, far_c))
    f32 = jnp.float32
    low = jnp.bfloat16
    scale = HDIM**-0.5
    for half in range(2):
        columns = slice(half * SPAN, (half + 1) * SPAN)
        q_rows = query[columns, :]
        g_rows = grad_out[columns, :]
        both = g_rows.astype(f32) * out[columns, :].astype(f32)
        delta = jnp.sum(both.T, axis=0, keepdims=True)
        log_row = log_total[:, columns]
        for span, kind in spans_of(half):
            rows = slice(span * SPAN, (span + 1) * SPAN)
            fresh = half == 1 and span >= 4 or half == 0

            def visit(rows=rows, span=span, kind=kind, fresh=fresh):
                k_rows, v_rows = key_rows(parts, span)
                logits = logits_of(k_rows, q_rows, kind, place[1])
                probs = jnp.exp(logits - log_row)
                grad_probs = lax.dot_general(
                    v_rows,
                    g_rows,
                    (((1,), (1,)), ((), ())),
                    preferred_element_type=f32,
                )
                grad_logits = (probs * (grad_probs - delta)).astype(low)
                grad_k = jnp.dot(grad_logits, q_rows, preferred_element_type=f32)
                grad_v = jnp.dot(probs.astype(low), g_rows, preferred_element_type=f32)
                if fresh:
                    sums[rows, 0:HDIM] = grad_k
                    sums[rows, HDIM:] = grad_v
                else:
                    sums[rows, 0:HDIM] += grad_k
                    sums[rows, HDIM:] += grad_v
                part = lax.dot_general(
                    k_rows, grad_logits, (((0,), (0,)), ((), ())), preferred_element_type=f32
                )
                wide[...] = part if kind == 0 else wide[...] + part

            if kind == 2:
                pl.when(place[0] == 1)(visit)

                @pl.when(place[0] == 0)
                def _(rows=rows):
                    sums[rows, :] = jnp.zeros((SPAN, 2 * HDIM), f32)
            else:
                visit()
        grad_query[columns, :] = (wide[...] * scale).T.astype(low)
    for xa in range(2):
        for cr, target in ((0, same_core), (1, other_core)):
            for xr in range(2):
                span = xa * 4 + cr * 2 + xr
                rows = slice(span * SPAN, (span + 1) * SPAN)
                target[xa, xr, :, 0:HDIM] = (sums[rows, 0:HDIM] * scale).astype(low)
                target[xa, xr, :, HDIM:] = sums[rows, HDIM:].astype(low)


def attend_back(place, query, kv, out, log_total, grad_out):
    vmem = pl.BlockSpec(memory_space=pltpu.VMEM)
    part = jax.ShapeDtypeStruct((2, 2, SPAN, 2 * HDIM), jnp.bfloat16)
    return pl.pallas_call(
        attend_back_kernel,
        in_specs=[pl.BlockSpec(memory_space=pltpu.SMEM)] + [vmem] * 8,
        out_shape=[jax.ShapeDtypeStruct(query.shape, jnp.bfloat16), part, part],
        scratch_shapes=[
            pltpu.VMEM((8 * SPAN, 2 * HDIM), jnp.float32),
            pltpu.VMEM((HDIM, SPAN), jnp.float32),
        ],
        compiler_params=pltpu.CompilerParams(vmem_limit_bytes=40 * 1024 * 1024),
        cost_estimate=pl.CostEstimate(
            flops=4000000000, bytes_accessed=6000000, transcendentals=3000000
        ),
    )(place, query, *kv, out, log_total, grad_out)


def both_sides(rows):
    return jnp.concatenate(
        [
            from_behind(rows[-FAR:], 2),
            from_behind(rows, 1),
            from_behind(rows, -1),
            from_behind(rows[:FAR], -2),
        ]
    )


def first_norm(residual, attention, w_out, norm_gain):
    x_float = residual.astype(jnp.float32) + jnp.dot(
        attention, w_out, preferred_element_type=jnp.float32
    )
    x_first = lax.optimization_barrier(x_float.astype(jnp.bfloat16))
    x_float = x_first.astype(jnp.float32)
    inv_rms = lax.rsqrt(jnp.mean(x_float * x_float, axis=-1, keepdims=True) + 1e-05)
    normed = lax.optimization_barrier((x_float * inv_rms * norm_gain).astype(jnp.bfloat16))
    return x_first, inv_rms, normed


def to_heads(rows_in):
    return rows_in.reshape(rows_in.shape[0], HEADS, HDIM).transpose(1, 0, 2)


def from_heads(pieces):
    return pieces.transpose(1, 0, 2).reshape(pieces.shape[1], HEADS * HDIM)


def gather_keys(own):
    far = swap(own, "xb")
    return own, far, swap(own, "c"), swap(far, "c")


def weight_pieces(attention, grad_residual):
    core = lax.axis_index("c")
    half = AD // 2
    mine = jnp.where(core == 0, attention[:, :half], attention[:, half:])
    theirs = jnp.where(core == 0, attention[:, half:], attention[:, :half])
    rows_a = jnp.concatenate([mine, swap(theirs, "c")], axis=0)
    rows_g = jnp.concatenate([grad_residual, swap(grad_residual, "c")], axis=0)
    peers = lax.axis_size("y")
    width = half // peers
    at = lax.axis_index("y")
    pieces = []
    for step in range(peers):
        columns = lax.dynamic_slice_in_dim(rows_a, (at + step) % peers * width, width, axis=1)
        piece = lax.dot_general(
            rows_g, columns, (((0,), (0,)), ((), ())), preferred_element_type=jnp.float32
        )
        pieces.append(piece.astype(jnp.bfloat16))
    return lax.optimization_barrier(pieces)


def over_y(pieces):
    peers = len(pieces)
    total = pieces[0].astype(jnp.float32)
    for step in range(1, peers):
        pairs = [(i, (i + step) % peers) for i in range(peers)]
        total = total + lax.ppermute(pieces[step], "y", pairs).astype(jnp.float32)
    return total


def all_over_y(part):
    peers = lax.axis_size("y")
    parts = [part]
    for step in range(1, peers):
        pairs = [(i, (i + step) % peers) for i in range(peers)]
        parts.append(lax.ppermute(part, "y", pairs))
    while len(parts) > 1:
        half = len(parts) // 2
        parts = [parts[i] + parts[i + half] for i in range(half)]
    return parts[0]


def over_zl_and_xb(total, small):
    zl = lax.axis_index("zl")
    xb = lax.axis_index("xb")
    total = total.astype(jnp.bfloat16).reshape(2, 2, 4, 2, D // 32, -1)
    width = total.shape[-1]
    small = small.astype(jnp.bfloat16).reshape(1, -1, width)
    total = jnp.where(xb == 0, total, total[:, ::-1])
    total = jnp.where(zl == 0, total, total[:, :, :, ::-1])
    received = None
    for turn in range(2):
        for move in range(2):
            piece = total[:, move, :, turn].reshape(1, -1, width)
            piece = jnp.concatenate([piece, small], axis=1)[0]
            pairs = [
                (a * 4 + x * 2 + b, b * 4 + (x ^ move) * 2 + (a ^ turn))
                for a in range(2)
                for x in range(2)
                for b in range(2)
            ]
            part = lax.ppermute(piece, ("zl", "xb", "c"), pairs).astype(jnp.float32)
            received = [part] if received is None else received + [part]
    total = (received[0] + received[1]) + (received[2] + received[3])
    rows = 8 * (D // 32)
    return total[:rows].astype(jnp.bfloat16).reshape(8, D // 32, width), total[rows:]


def local(
    query_in,
    key_in,
    value_in,
    residual,
    w_out,
    norm_gain,
    short_taps,
    filters,
    skip_gain,
    cotangent,
):
    tok_rows = query_in.shape[1]
    matrices = toeplitz(filters)
    qkv_send = jnp.concatenate(
        [to_heads(query_in[0]), to_heads(key_in[0]), to_heads(value_in[0])], axis=1
    )
    qkv_own = exchange(qkv_send, HEAD_AXES)
    query_rows = qkv_own[:, :tok_rows].reshape(8 * tok_rows, HDIM)
    kv_all = gather_keys(qkv_own[:, tok_rows:])
    cot_sides = (from_behind(cotangent[0], -1), from_behind(cotangent[0, :FAR], -2))
    query_total = 8 * tok_rows
    place = jnp.stack([lax.axis_index("xb"), lax.axis_index("c")]).astype(jnp.int32)
    head_out, log_total = attend(place, query_rows, kv_all)
    head_out, cot_sides = lax.optimization_barrier((head_out, cot_sides))
    attention = from_heads(exchange(head_out.reshape(8, tok_rows, HDIM), HEAD_AXES))
    x_first, inv_rms, normed = first_norm(residual[0], attention, w_out, norm_gain)
    sides = both_sides(normed)
    layer_out, grad_residual, small = hyena(
        normed,
        sides,
        x_first,
        cotangent[0],
        cot_sides,
        inv_rms,
        short_taps,
        norm_gain,
        skip_gain,
        matrices,
    )

    grad_attention = jnp.einsum(
        "td,ad->ta", grad_residual, w_out, preferred_element_type=jnp.float32
    ).astype(jnp.bfloat16)
    small_rows = (FILTERS + 1) * SMALL // 8
    small_send = small.reshape(8, small_rows, HDIM).astype(jnp.bfloat16)
    grad_recv = exchange(
        jnp.concatenate([to_heads(grad_attention), small_send], axis=1), HEAD_AXES
    )
    pieces = weight_pieces(attention, grad_residual)
    weight_part = over_y(pieces)
    grad_rows_all = grad_recv[:, :tok_rows].reshape(query_total, HDIM)
    small_part = jnp.sum(grad_recv[:, tok_rows:].astype(jnp.float32), axis=0)
    grad_query, same_core, other_core = attend_back(
        place, query_rows, kv_all, head_out, log_total, grad_rows_all
    )
    small_part, _ = lax.optimization_barrier((small_part, grad_query))
    small_part = all_over_y(small_part + swap(small_part, "c"))
    grad_query = exchange(grad_query.reshape(8, tok_rows, HDIM), HEAD_AXES)
    dkv = same_core.astype(jnp.float32) + swap(other_core, "c").astype(jnp.float32)
    dkv_far = swap(dkv[:, 1].astype(jnp.bfloat16), "xb")
    dkv = dkv[:, 0] + dkv_far.astype(jnp.float32)
    dkv = dkv.reshape(8, tok_rows, 2 * HDIM).astype(jnp.bfloat16)
    weight_part, _ = lax.optimization_barrier((weight_part, grad_query))
    weight_part, small_part = over_zl_and_xb(weight_part, small_part)
    small_part = small_part.reshape(-1, HDIM).astype(jnp.bfloat16)
    weight_rows = weight_part.size // (8 * HDIM)
    last_send = jnp.concatenate(
        [
            dkv[:, :, :HDIM],
            dkv[:, :, HDIM:],
            jnp.broadcast_to(small_part[None], (8,) + small_part.shape),
            weight_part.reshape(8, weight_rows, HDIM),
        ],
        axis=1,
    )
    last = exchange(last_send, HEAD_AXES)
    grad_query = from_heads(grad_query)
    grad_key = from_heads(last[:, :tok_rows])
    grad_value = from_heads(last[:, tok_rows : 2 * tok_rows])
    sums_back = last[:, 2 * tok_rows :].astype(jnp.float32)
    small_back = sums_back[:, :small_rows]
    small_back = small_back.reshape(FILTERS + 1, SMALL, FCH)[:FILTERS].transpose(1, 0, 2)
    grad_filters = small_back[SMALL - 1]
    small_back = small_back.reshape(SMALL, D)
    grad_weight = jnp.sum(sums_back[:, small_rows:], axis=0)
    grad_weight = grad_weight.reshape(D // 32, -1).T
    return (
        layer_out[None],
        grad_residual[None],
        grad_query[None],
        grad_key[None],
        grad_value[None],
        grad_weight,
        small_back[3 * SHORT],
        small_back[: 3 * SHORT].reshape(3, SHORT, D),
        grad_filters,
        small_back[3 * SHORT + 1],
    )


def solution(mesh):
    sequences = mesh.shape["dp"]
    split = Mesh(
        mesh.devices.reshape(2, sequences // 2, 2, 2, 4, 2), DP_AXES + CTX_AXES
    )
    rows = P(DP_AXES, CTX_AXES, None)
    in_specs = (rows, rows, rows, rows, P(), P(), P(), P(), P(), rows)
    out_specs = (rows, rows, rows, rows, rows, P(DP_AXES, CTX_AXES), P(), P(), P(), P())
    return jax.shard_map(local, mesh=split, in_specs=in_specs, out_specs=out_specs, check_vma=False)
```
